256 devices in a mesh: dp: 16 (over z, y_hi), expert: 16 (over y_lo, x, core).
Axes of the slice: x: 4, y: 4 (y_hi: 2, y_lo: 2; y = y_hi * 2 + y_lo), z: 8, core: 2. Of those that a mesh axis runs over, the one named last changes fastest.
Arguments:
- tokens: bfloat16 [65536, 1024], P(('dp', 'expert')), may hold values from -6 to 6
- token_picks: int32 [256, 16, 32], P(('dp', 'expert')), may hold values from 0 to 255, as said below
- gate_values: float32 [256, 16, 32], P(('dp', 'expert')), may hold values from 0.05 to 1
- w_in: bfloat16 [16, 1024, 2048], P('expert'), may hold values from -0.1875 to 0.1875
- w_out: bfloat16 [16, 2048, 1024], P('expert'), may hold values from -0.125 to 0.125
- cotangent: bfloat16 [65536, 1024], P(('dp', 'expert')), may hold values from -24 to 24
Outputs:
- mixed: bfloat16 [65536, 1024], P(('dp', 'expert'))
- token_grad: bfloat16 [65536, 1024], P(('dp', 'expert'))
- grad_in: bfloat16 [1024, 16, 2048], P('dp', 'expert')
- grad_out: bfloat16 [1024, 16, 2048], P('dp', 'expert')
The draws below stay inside these ranges and needn't reach their ends.
Inputs may be any that keep to these rules, and one draw needn't show every extreme that they name: `token_picks`: entry (i, e, p) is one of device i's 256 local token rows that expert e takes; for each device and expert the 32 rows are distinct.
All inputs are finite; a program needn't handle non-finite values.
Results may differ from the reference program's by a relative error of at most 0.024.
Values may be sent and summed in bfloat16 or wider, within the bound.
A program may use at most 128 MiB of HBM per device.

```python
import math
import jax
import jax.numpy as jnp
from jax import lax

D = 1024
H = 2048
TOK_DEV = 256
EXPERTS = 16
PICK = 32
TOKENS = 65536
N_DP = 16
N_EXPERT = 16


def draw_token_picks(key, part):
    key = jax.random.fold_in(key, 11)
    scores = jax.random.randint(key, (N_DP * N_EXPERT, EXPERTS, TOK_DEV), 0, 1 << 20)
    scores = scores * TOK_DEV + jnp.arange(TOK_DEV, dtype=jnp.int32)[None, None, :]
    order = jnp.argsort(scores, axis=-1, stable=True)
    return order[:, :, :PICK].astype(jnp.int32)


def strengthened(drawn, rng, source, target, shards_of, factor):
    owner, partner = [(jnp.arange(drawn.shape[position]) // (drawn.shape[position] // shards_of)).reshape([-1 if axis == position else 1 for axis in range(drawn.ndim)]) for position in (source, target)]
    chosen = jax.random.permutation(rng, shards_of)[partner]
    strong = (owner == chosen) | (owner == (partner + shards_of // 2) % shards_of)
    return jnp.where(strong, factor * drawn, drawn)


def levels(key, shape, cuts, least, top_value):
    factor_of, own = 1.0, jax.random.fold_in(key, 6)
    for dim, parts in cuts:
        draws = jnp.exp(jax.random.uniform(jax.random.fold_in(own, dim), (parts,), jnp.float32, least / len(cuts), top_value / len(cuts)))
        factor_of = factor_of * jnp.repeat(draws, shape[dim] // parts).reshape([-1 if axis == dim else 1 for axis in range(len(shape))])
    return factor_of


def bell_draw(stream_key, shape, scale, limit, pieces=(), held_as=jnp.bfloat16):
    values = jax.random.normal(stream_key, shape, jnp.float32) * scale
    if len(pieces) > 0:
        values = levels(stream_key, shape, pieces, -0.22, 0.18) * values
    return jnp.clip(values, min=-limit, max=limit).astype(held_as)


def gaussian_with(key, extent, deviation, bound, pieces, heavy, kind=jnp.bfloat16):
    result = deviation * jax.random.normal(key, extent, jnp.float32)
    if pieces:
        result = result * levels(key, extent, pieces, -0.22, 0.18)
    return jnp.clip(strengthened(result, jax.random.fold_in(key, 3), *heavy), -bound, bound).astype(kind)


def setup_inputs(seed: int = 0) -> dict:
    key_of = jax.random.split(jax.random.key(seed), 7)
    return {
        "tokens": bell_draw(key_of[0], (TOKENS, D), 1.0, 6.0, ((0, 256),)),
        "token_picks": draw_token_picks(jax.random.fold_in(key_of[6], 71), 0),
        "gate_values": jnp.clip(jnp.exp(math.log(1.0) - 2.9957323 * jax.random.uniform(key_of[2], (N_DP * N_EXPERT, EXPERTS, PICK), jnp.float32) ** levels(key_of[2], (N_DP * N_EXPERT, EXPERTS, PICK), ((0, 256),), -0.2, 0.2)), 0.05, 1.0),
        "w_in": bell_draw(key_of[3], (EXPERTS, D, H), D ** -0.5, 0.1875, ((0, 16),)),
        "w_out": bell_draw(key_of[4], (EXPERTS, H, D), H ** -0.5, 0.125, ((0, 16),)),
        "cotangent": gaussian_with(key_of[5], (TOKENS, D), 1.0, 24.0, ((0, 256),), (0, 1, 256, 6.0)),
    }


def gelu_exact(values):
    return jax.nn.gelu(values, approximate=False)

def reference(tokens, token_picks, gate_values, w_in, w_out, cotangent):
    devices = token_picks.shape[0]
    local_tokens = tokens.shape[0] // devices
    width = tokens.shape[1]
    hidden = w_in.shape[2]
    offsets = jnp.arange(devices, dtype=jnp.int32) * local_tokens
    rows_all = token_picks + offsets[:, None, None]
    rows_by_expert = jnp.swapaxes(rows_all, 0, 1)
    gates_by_expert = jnp.swapaxes(gate_values, 0, 1)

    def expert_work(operands):
        picked, gate_rows, w_first, w_second = operands
        flat_index = picked.reshape(-1)
        gate_flat = gate_rows.reshape(-1)
        taken = jnp.take(tokens, flat_index, axis=0)
        pre_act = jnp.dot(taken, w_first, preferred_element_type=jnp.float32)
        act_f, gelu_back = jax.vjp(gelu_exact, pre_act)
        activated = act_f.astype(jnp.bfloat16)
        expert_out = jnp.dot(activated, w_second, preferred_element_type=jnp.float32).astype(jnp.bfloat16)
        grad_sent = (jnp.take(cotangent, flat_index, axis=0).astype(jnp.float32) * gate_flat[:, None]).astype(jnp.bfloat16)
        grad_act = jnp.dot(grad_sent, w_second.T, preferred_element_type=jnp.float32)
        grad_pre = gelu_back(grad_act)[0].astype(jnp.bfloat16)
        grad_taken = jnp.dot(grad_pre, w_first.T, preferred_element_type=jnp.float32).astype(jnp.bfloat16)
        taken_groups = taken.reshape(N_DP, -1, width).astype(jnp.float32)
        pre_groups = grad_pre.reshape(N_DP, -1, hidden).astype(jnp.float32)
        sent_groups = grad_sent.reshape(N_DP, -1, width).astype(jnp.float32)
        act_groups = activated.reshape(N_DP, -1, hidden).astype(jnp.float32)
        part_in = jnp.einsum('rkd,rkh->rdh', taken_groups, pre_groups).astype(jnp.bfloat16)
        part_out = jnp.einsum('rkd,rkh->rdh', sent_groups, act_groups).astype(jnp.bfloat16)
        sum_in = lax.optimization_barrier(jnp.sum(part_in.astype(jnp.float32), axis=0)).astype(jnp.bfloat16)
        sum_out = lax.optimization_barrier(jnp.sum(part_out.astype(jnp.float32), axis=0)).astype(jnp.bfloat16)
        return (expert_out, grad_taken, sum_in, sum_out)
    outs_e, grads_e, sums_in, sums_out = lax.map(expert_work, (rows_by_expert, gates_by_expert, w_in, w_out))
    all_rows = rows_by_expert.reshape(-1)
    weighted = outs_e.astype(jnp.float32) * gates_by_expert.reshape(gates_by_expert.shape[0], -1)[:, :, None]
    mixed = jnp.zeros(tokens.shape, jnp.float32).at[all_rows].add(weighted.reshape(-1, width)).astype(jnp.bfloat16)
    token_grad = jnp.zeros(tokens.shape, jnp.float32).at[all_rows].add(grads_e.reshape(-1, width).astype(jnp.float32)).astype(jnp.bfloat16)
    grad_in = jnp.transpose(sums_in, (1, 0, 2))
    grad_out = jnp.transpose(sums_out, (1, 0, 2))
    return (mixed, token_grad, grad_in, grad_out)
```

```python
import functools

import jax
import jax.numpy as jnp
from jax import lax
from jax.experimental import pallas as pl
from jax.experimental.pallas import tpu as pltpu
from jax.sharding import PartitionSpec as P

MESH = pl.DeviceIdType.MESH
BF = jnp.bfloat16
F32 = jnp.float32
NT = (((1,), (1,)), ((), ()))


def dot(a, b):
    return jnp.dot(a, b, preferred_element_type=F32)


def dot_nt(a, b):
    return lax.dot_general(a, b, NT, preferred_element_type=F32)


def kernel(
    n_dp, n_ex,
    tok, pick, gate, win_hbm, wout_hbm, cot,
    mixed, tgrad, gin, gout,
    win, wout, stok, sgrad, taken, gsent, act, dgel, gpre, eout, gtak, rout, rgrad,
    xt, part, ring, ysend, yrecv,
    wsem, dsend, drecv, rsend, rrecv, ysem_s, ysem_r,
):
    nz = n_dp // 2
    tokens, width = tok.shape
    per = pick.shape[2]
    rows = n_ex * per
    hidden = win.shape[1]
    blk = width // nz
    half_rows = blk // 2
    half = hidden // 2
    r = lax.axis_index("dp")
    me = lax.axis_index("expert")
    z = r // 2
    yh = r % 2
    up = (r + 2) % n_dp
    down = (r + n_dp - 2) % n_dp
    across = r + 1 - 2 * yh

    barrier = pltpu.get_barrier_semaphore()

    def greet(k, c):
        pl.semaphore_signal(
            barrier, inc=1, device_id={"expert": (me + k) % n_ex}, device_id_type=MESH
        )
        return c

    lax.fori_loop(1, n_ex, greet, 0)
    for other in (up, down, across):
        pl.semaphore_signal(barrier, inc=1, device_id={"dp": other}, device_id_type=MESH)

    load_in = pltpu.make_async_copy(win_hbm.at[0], win, wsem.at[0])
    load_out = pltpu.make_async_copy(wout_hbm.at[0], wout, wsem.at[1])
    load_in.start()
    load_out.start()

    p2 = pick[0].astype(F32).astype(BF)
    g = gate[0]
    g1 = g.astype(BF)
    g2 = (g - g1.astype(F32)).astype(BF)
    g3 = (g - g1.astype(F32) - g2.astype(F32)).astype(BF)
    row_e = lax.broadcasted_iota(jnp.int32, (rows, n_ex), 0) // per
    expert_of = (row_e == lax.broadcasted_iota(jnp.int32, (rows, n_ex), 1)).astype(F32).astype(BF)
    place = lax.broadcasted_iota(jnp.int32, (rows, per), 0) % per
    here = place == lax.broadcasted_iota(jnp.int32, (rows, per), 1)

    def column(values):
        return jnp.sum(jnp.where(here, values, 0.0), axis=1, keepdims=True)

    pick_col = column(dot(expert_of, p2))
    gate_col = column(dot(expert_of, g1) + dot(expert_of, g2) + dot(expert_of, g3))
    lanes = lax.broadcasted_iota(jnp.int32, (rows, tokens), 1).astype(F32)
    sel = (lanes == pick_col).astype(F32).astype(BF)
    spread = dot_nt(p2, here.astype(F32).astype(BF))
    own_e = lax.broadcasted_iota(jnp.int32, (n_ex, rows), 0) == (
        lax.broadcasted_iota(jnp.int32, (n_ex, rows), 1) // per
    )
    pick_row = jnp.sum(jnp.where(own_e, spread, 0.0), axis=0, keepdims=True)
    selt = lax.broadcasted_iota(jnp.int32, (tokens, rows), 0).astype(F32) == pick_row
    gspread = (
        dot_nt(g1, here.astype(F32).astype(BF))
        + dot_nt(g2, here.astype(F32).astype(BF))
        + dot_nt(g3, here.astype(F32).astype(BF))
    )
    gate_row = jnp.sum(jnp.where(own_e, gspread, 0.0), axis=0, keepdims=True)

    stok[...] = dot(sel, tok[...]).astype(BF)

    pl.semaphore_wait(barrier, n_ex + 2)

    def exchange(which, src, dst, peer):
        return pltpu.make_async_remote_copy(
            src_ref=src.at[pl.ds(peer * per, per)],
            dst_ref=dst.at[pl.ds(me * per, per)],
            send_sem=dsend.at[which, peer],
            recv_sem=drecv.at[which, me],
            device_id={"expert": peer},
            device_id_type=MESH,
        )

    def send_all(which, src, dst):
        def body(i, c):
            k = 1 + i // 2
            peer = (me + k * (1 - 2 * (i % 2)) + n_ex) % n_ex
            exchange(which, src, dst, peer).start()
            return c

        lax.fori_loop(0, n_ex - 1, body, 0)
        own = pl.ds(me * per, per)
        dst[own, :] = src[own, :]

    def recv_all(which, src, dst):
        def body(k, c):
            peer = (me + k) % n_ex
            pltpu.make_async_remote_copy(
                src_ref=src.at[pl.ds(peer * per, per)],
                dst_ref=dst.at[pl.ds(peer * per, per)],
                send_sem=dsend.at[which, peer],
                recv_sem=drecv.at[which, peer],
                device_id={"expert": peer},
                device_id_type=MESH,
            ).wait_recv()
            return c

        lax.fori_loop(1, n_ex, body, 0)

    def sent_all(which, src, dst):
        def body(k, c):
            exchange(which, src, dst, (me + k) % n_ex).wait_send()
            return c

        lax.fori_loop(1, n_ex, body, 0)

    send_all(0, stok, taken)
    sgrad[...] = (dot(sel, cot[...]) * gate_col).astype(BF)
    send_all(1, sgrad, gsent)

    load_in.wait()
    recv_all(0, stok, taken)

    tile = min(256, hidden)

    def forward(j, c):
        cols = pl.ds(pl.multiple_of(j * tile, tile), tile)
        pre = dot(taken[...], win[:, cols])
        cdf = 0.5 * (1.0 + lax.erf(pre * 0.7071067811865476))
        act[:, cols] = (pre * cdf).astype(BF)
        dgel[:, cols] = cdf + pre * (0.3989422804014327 * jnp.exp(-0.5 * pre * pre))
        return c

    lax.fori_loop(0, hidden // tile, forward, 0)
    xt[1] = taken[...].T

    load_out.wait()
    wtile = min(256, width)

    def out_proj(j, c):
        cols = pl.ds(pl.multiple_of(j * wtile, wtile), wtile)
        eout[:, cols] = dot(act[...], wout[:, cols]).astype(BF)
        return c

    lax.fori_loop(0, width // wtile, out_proj, 0)
    send_all(2, eout, rout)

    recv_all(1, sgrad, gsent)

    def backward(j, c):
        cols = pl.ds(pl.multiple_of(j * tile, tile), tile)
        gact = dot_nt(gsent[...], wout[cols, :])
        gpre[:, cols] = (gact * dgel[:, cols]).astype(BF)
        return c

    lax.fori_loop(0, hidden // tile, backward, 0)
    xt[0] = gsent[...].T

    def hop(m, d, t):
        return pltpu.make_async_remote_copy(
            src_ref=ring.at[m, d, t],
            dst_ref=ring.at[m, d, t + 1],
            send_sem=rsend.at[m, d, t],
            recv_sem=rrecv.at[m, d, t + 1],
            device_id={"dp": (up, down)[d]},
            device_id_type=MESH,
        )

    def arrived(m, d, t):
        pltpu.make_async_remote_copy(
            src_ref=ring.at[m, d, t],
            dst_ref=ring.at[m, d, t],
            send_sem=rsend.at[m, d, t - 1],
            recv_sem=rrecv.at[m, d, t],
            device_id={"dp": (up, down)[d]},
            device_id_type=MESH,
        ).wait_recv()

    def local_part(m, d, t):
        b = (z + nz - 1 - t) % nz if d == 0 else (z + 1 + t) % nz
        left = xt[m, pl.ds(pl.multiple_of(b * blk, blk), blk), :]
        other = (act, gpre)[m]
        return dot(left, other[:, d * half : (d + 1) * half])

    for m in (0, 1):
        for d in (0, 1):
            ring[m, d, 0] = local_part(m, d, 0).astype(BF)
            hop(m, d, 0).start()

    def grad_tokens(j, c):
        cols = pl.ds(pl.multiple_of(j * wtile, wtile), wtile)
        gtak[:, cols] = dot_nt(gpre[...], win[cols, :]).astype(BF)
        return c

    lax.fori_loop(0, width // wtile, grad_tokens, 0)
    send_all(3, gtak, rgrad)

    def ring_step(t, c):
        for m in (0, 1):
            for d in (0, 1):
                part[...] = local_part(m, d, t)
                arrived(m, d, t)
                ring[m, d, t] = (part[...] + ring[m, d, t].astype(F32)).astype(BF)
                hop(m, d, t).start()
        return c

    middle = min(5, nz - 1)
    lax.fori_loop(1, middle, ring_step, 0)

    recv_all(2, eout, rout)
    hi = gate_row.astype(BF).astype(F32)
    mixed[...] = (
        dot(jnp.where(selt, hi, 0.0).astype(BF), rout[...])
        + dot(jnp.where(selt, gate_row - hi, 0.0).astype(BF), rout[...])
    ).astype(BF)
    recv_all(3, gtak, rgrad)
    tgrad[...] = dot(selt.astype(F32).astype(BF), rgrad[...]).astype(BF)

    lax.fori_loop(middle, nz - 1, ring_step, 0)

    keep = pl.multiple_of(yh * half_rows, half_rows)
    give = pl.multiple_of((1 - yh) * half_rows, half_rows)

    def swap(m, d):
        return pltpu.make_async_remote_copy(
            src_ref=ysend.at[m, d],
            dst_ref=yrecv.at[m, d],
            send_sem=ysem_s.at[m, d],
            recv_sem=ysem_r.at[m, d],
            device_id={"dp": across},
            device_id_type=MESH,
        )

    for m in (0, 1):
        for d in (0, 1):
            part[...] = local_part(m, d, nz - 1)
            arrived(m, d, nz - 1)
            part[...] = part[...] + ring[m, d, nz - 1].astype(F32)
            ysend[m, d] = part[pl.ds(give, half_rows), :].astype(BF)
            swap(m, d).start()
            out = (gout, gin)[m]
            out[:, d * half : (d + 1) * half] = part[pl.ds(keep, half_rows), :].astype(BF)
    for m in (0, 1):
        for d in (0, 1):
            swap(m, d).wait()
            out = (gout, gin)[m]
            cols = slice(d * half, (d + 1) * half)
            out[:, cols] = (out[:, cols].astype(F32) + yrecv[m, d].astype(F32)).astype(BF)

    for which, src, dst in ((0, stok, taken), (1, sgrad, gsent), (2, eout, rout), (3, gtak, rgrad)):
        sent_all(which, src, dst)

    def ring_sent(t, c):
        for m in (0, 1):
            for d in (0, 1):
                hop(m, d, t).wait_send()
        return c

    lax.fori_loop(0, nz - 1, ring_sent, 0)


def on_device(n_dp, n_ex, tokens, picks, gates, w_in, w_out, cotangent):
    count, width = tokens.shape
    hidden = w_in.shape[2]
    per = picks.shape[2]
    rows = n_ex * per
    nz = n_dp // 2
    blk = width // nz
    half = hidden // 2
    vmem = pl.BlockSpec(memory_space=pltpu.VMEM)
    hbm = pl.BlockSpec(memory_space=pl.ANY)
    mixed, tgrad, gin, gout = pl.pallas_call(
        functools.partial(kernel, n_dp, n_ex),
        out_shape=(
            jax.ShapeDtypeStruct((count, width), BF),
            jax.ShapeDtypeStruct((count, width), BF),
            jax.ShapeDtypeStruct((width // n_dp, hidden), BF),
            jax.ShapeDtypeStruct((width // n_dp, hidden), BF),
        ),
        in_specs=[vmem, vmem, vmem, hbm, hbm, vmem],
        out_specs=(vmem, vmem, vmem, vmem),
        scratch_shapes=[
            pltpu.VMEM((width, hidden), BF),
            pltpu.VMEM((hidden, width), BF),
            pltpu.VMEM((rows, width), BF),
            pltpu.VMEM((rows, width), BF),
            pltpu.VMEM((rows, width), BF),
            pltpu.VMEM((rows, width), BF),
            pltpu.VMEM((rows, hidden), BF),
            pltpu.VMEM((rows, hidden), F32),
            pltpu.VMEM((rows, hidden), BF),
            pltpu.VMEM((rows, width), BF),
            pltpu.VMEM((rows, width), BF),
            pltpu.VMEM((rows, width), BF),
            pltpu.VMEM((rows, width), BF),
            pltpu.VMEM((2, width, rows), BF),
            pltpu.VMEM((blk, half), F32),
            pltpu.VMEM((2, 2, nz, blk, half), BF),
            pltpu.VMEM((2, 2, blk // 2, half), BF),
            pltpu.VMEM((2, 2, blk // 2, half), BF),
            pltpu.SemaphoreType.DMA((2,)),
            pltpu.SemaphoreType.DMA((4, n_ex)),
            pltpu.SemaphoreType.DMA((4, n_ex)),
            pltpu.SemaphoreType.DMA((2, 2, nz)),
            pltpu.SemaphoreType.DMA((2, 2, nz)),
            pltpu.SemaphoreType.DMA((2, 2)),
            pltpu.SemaphoreType.DMA((2, 2)),
        ],
        compiler_params=pltpu.CompilerParams(
            collective_id=0, has_side_effects=True, vmem_limit_bytes=58 * 1024 * 1024
        ),
        cost_estimate=pl.CostEstimate(
            flops=12 * rows * width * hidden,
            bytes_accessed=4 * width * hidden + 8 * count * width,
            transcendentals=2 * rows * hidden,
        ),
    )(tokens, picks, gates, w_in, w_out, cotangent)
    return mixed, tgrad, gin[:, None, :], gout[:, None, :]


def solution(mesh):
    n_dp, n_ex = mesh.shape["dp"], mesh.shape["expert"]
    in_specs = (
        P(("dp", "expert"), None),
        P(("dp", "expert"), None, None),
        P(("dp", "expert"), None, None),
        P("expert", None, None),
        P("expert", None, None),
        P(("dp", "expert"), None),
    )
    out_specs = (
        P(("dp", "expert"), None),
        P(("dp", "expert"), None),
        P("dp", "expert", None),
        P("dp", "expert", None),
    )
    return jax.shard_map(
        functools.partial(on_device, n_dp, n_ex),
        mesh=mesh,
        in_specs=in_specs,
        out_specs=out_specs,
        check_vma=False,
    )
```

```python
import functools

import jax
import jax.numpy as jnp
from jax import lax
from jax.experimental import pallas as pl
from jax.experimental.pallas import tpu as pltpu
from jax.sharding import PartitionSpec as P

MESH = pl.DeviceIdType.MESH
BF = jnp.bfloat16
F32 = jnp.float32
NT = (((1,), (1,)), ((), ()))
ZC = 4


def dot(a, b):
    return jnp.dot(a, b, preferred_element_type=F32)


def dot_nt(a, b):
    return lax.dot_general(a, b, NT, preferred_element_type=F32)


def kernel(
    n_dp, n_ex, zc,
    tok_hbm, pick, gate, win_hbm, wout_hbm, cot_hbm,
    mixed, tgrad, gin, gout,
    win, wout, tok, cot, stok, sgrad, taken, gsent, gflat, act, dgel, gpre, eout, gtak, rout, rgrad,
    xt, part, ring_o, ring_i, ring_y, ykeep, ysend, yrecv,
    fin_o, fin_i, swap_so, swap_ro, swap_si, swap_ri,
    wsem, tsend, trecv, gsend, grecv,
    osend, orecv, isend, irecv, rysend, ryrecv, xsend, xrecv,
    sosend, sorecv, sisend, sirecv,
):
    nz = n_dp // 2
    tokens, width = tok.shape
    per = pick.shape[2]
    rows = n_ex * per
    hidden = win.shape[1]
    blk = width // nz
    half_rows = blk // 2
    half = hidden // 2
    yc = half - zc
    r = lax.axis_index("dp")
    me = lax.axis_index("expert")
    z = r // 2
    yh = r % 2
    up = (r + 2) % n_dp
    down = (r + n_dp - 2) % n_dp
    across = r + 1 - 2 * yh

    loads = [
        pltpu.make_async_copy(src, dst, wsem.at[i])
        for i, (src, dst) in enumerate(
            ((tok_hbm, tok), (cot_hbm, cot), (win_hbm.at[0], win), (wout_hbm.at[0], wout))
        )
    ]
    for load in loads:
        load.start()

    barrier = pltpu.get_barrier_semaphore()

    def greet(k, c):
        pl.semaphore_signal(
            barrier, inc=1, device_id={"expert": (me + k) % n_ex}, device_id_type=MESH
        )
        return c

    lax.fori_loop(1, n_ex, greet, 0)
    for other in (up, down, across):
        pl.semaphore_signal(barrier, inc=1, device_id={"dp": other}, device_id_type=MESH)

    p2 = pick[0].astype(F32).astype(BF)
    g = gate[0]
    g1 = g.astype(BF)
    g2 = (g - g1.astype(F32)).astype(BF)
    g3 = (g - g1.astype(F32) - g2.astype(F32)).astype(BF)
    row_e = lax.broadcasted_iota(jnp.int32, (rows, n_ex), 0) // per
    expert_of = (row_e == lax.broadcasted_iota(jnp.int32, (rows, n_ex), 1)).astype(F32).astype(BF)
    place = lax.broadcasted_iota(jnp.int32, (rows, per), 0) % per
    here = place == lax.broadcasted_iota(jnp.int32, (rows, per), 1)

    def column(values):
        return jnp.sum(jnp.where(here, values, 0.0), axis=1, keepdims=True)

    pick_col = column(dot(expert_of, p2))
    lanes = lax.broadcasted_iota(jnp.int32, (rows, tokens), 1).astype(F32)
    sel = (lanes == pick_col).astype(F32).astype(BF)
    loads[0].wait()
    stok[...] = dot(sel, tok[...]).astype(BF)

    def block_at(q):
        if q == nz - 1:
            return z
        if q == nz - 2:
            return (z + nz // 2) % nz
        return (z + 1 + q // 2) % nz if q % 2 else (z + nz - 1 - q // 2) % nz

    def order(d, t):
        if t == nz - 1:
            return nz - 1
        if t == nz // 2 - 1:
            return nz - 2
        if t < nz // 2:
            return 2 * t + d
        return 2 * (nz - 1 - t) - 1 - d

    def late(d, t):
        return 2 * (nz - 1 - t) - 1 - d

    def lane_block(b):
        return pl.ds(pl.multiple_of(b * blk, blk), blk)

    pl.semaphore_wait(barrier, n_ex + 2)

    def exchange(which, src, dst, peer, slot):
        return pltpu.make_async_remote_copy(
            src_ref=src.at[pl.ds(peer * per, per)],
            dst_ref=dst.at[pl.ds(slot * per, per)],
            send_sem=tsend.at[which, peer],
            recv_sem=trecv.at[which, slot],
            device_id={"expert": peer},
            device_id_type=MESH,
        )

    def peer_of(i):
        return (me + n_ex // 2 + (1 + i // 2) * (1 - 2 * (i % 2)) + n_ex) % n_ex

    def send_all(which, src, dst):
        exchange(which, src, dst, (me + n_ex // 2) % n_ex, me).start()

        def body(i, c):
            exchange(which, src, dst, peer_of(i), me).start()
            return c

        lax.fori_loop(0, n_ex - 2, body, 0)
        own = pl.ds(me * per, per)
        dst[own, :] = src[own, :]

    def recv_all(which, src, dst):
        def body(k, c):
            peer = (me + k) % n_ex
            exchange(which, src, dst, peer, peer).wait_recv()
            return c

        lax.fori_loop(1, n_ex, body, 0)

    def sent_all(which, src, dst):
        def body(k, c):
            exchange(which, src, dst, (me + k) % n_ex, me).wait_send()
            return c

        lax.fori_loop(1, n_ex, body, 0)

    def grad_chunk(i, peer, slot):
        return pltpu.make_async_remote_copy(
            src_ref=sgrad.at[pl.ds(2 * i, 2), pl.ds(peer * per, per)],
            dst_ref=gsent.at[pl.ds(2 * i, 2), pl.ds(slot * per, per)],
            send_sem=gsend.at[i, peer],
            recv_sem=grecv.at[i, slot],
            device_id={"expert": peer},
            device_id_type=MESH,
        )

    def send_grads(i, c):
        grad_chunk(i, (me + n_ex // 2) % n_ex, me).start()

        def body(k, c):
            grad_chunk(i, peer_of(k), me).start()
            return c

        lax.fori_loop(0, n_ex - 2, body, 0)
        return c

    def recv_grads(i):
        def body(k, c):
            peer = (me + k) % n_ex
            grad_chunk(i, peer, peer).wait_recv()
            return c

        lax.fori_loop(1, n_ex, body, 0)

    send_all(0, stok, taken)
    gate_col = column(dot(expert_of, g1) + dot(expert_of, g2) + dot(expert_of, g3))
    loads[1].wait()
    for q in range(nz):
        sgrad[q] = (dot(sel, cot[:, lane_block(block_at(q))]) * gate_col).astype(BF)
    lax.fori_loop(0, nz // 2, send_grads, 0)
    mine = pl.ds(me * per, per)
    for q in range(nz):
        gsent[q, mine, :] = sgrad[q, mine, :]

    here_bf = here.astype(F32).astype(BF)
    own_e = lax.broadcasted_iota(jnp.int32, (n_ex, rows), 0) == (
        lax.broadcasted_iota(jnp.int32, (n_ex, rows), 1) // per
    )

    def as_row(values):
        return jnp.sum(jnp.where(own_e, values, 0.0), axis=0, keepdims=True)

    pick_row = as_row(dot_nt(p2, here_bf))
    gate_row = as_row(dot_nt(g1, here_bf) + dot_nt(g2, here_bf) + dot_nt(g3, here_bf))

    tile = min(256, hidden)
    wtile = min(256, width)

    def forward(j, c):
        cols = pl.ds(pl.multiple_of(j * tile, tile), tile)
        pre = dot(taken[...], win[:, cols])
        cdf = 0.5 * (1.0 + lax.erf(pre * 0.7071067811865476))
        act[:, cols] = (pre * cdf).astype(BF)
        dgel[:, cols] = cdf + pre * (0.3989422804014327 * jnp.exp(-0.5 * pre * pre))
        return c

    def out_proj(j, c):
        cols = pl.ds(pl.multiple_of(j * wtile, wtile), wtile)
        eout[:, cols] = dot(act[...], wout[:, cols]).astype(BF)
        return c

    def backward(j, c):
        cols = pl.ds(pl.multiple_of(j * tile, tile), tile)
        gact = dot_nt(gflat[...], wout[cols, :])
        gpre[:, cols] = (gact * dgel[:, cols]).astype(BF)
        return c

    def grad_tokens(j, c):
        cols = pl.ds(pl.multiple_of(j * wtile, wtile), wtile)
        gtak[:, cols] = dot_nt(gpre[...], win[cols, :]).astype(BF)
        return c

    def hop(ring, ssem, rsem, d, j, t):
        return pltpu.make_async_remote_copy(
            src_ref=ring.at[d, j, t],
            dst_ref=ring.at[d, j, t + 1],
            send_sem=ssem.at[d, j, t],
            recv_sem=rsem.at[d, j, t + 1],
            device_id={"dp": (up, down)[d]},
            device_id_type=MESH,
        )

    def arrived(ring, ssem, rsem, d, j, t):
        pltpu.make_async_remote_copy(
            src_ref=ring.at[d, j, t],
            dst_ref=ring.at[d, j, t],
            send_sem=ssem.at[d, j, t - 1],
            recv_sem=rsem.at[d, j, t],
            device_id={"dp": (up, down)[d]},
            device_id_type=MESH,
        ).wait_recv()

    def block_of(d, t):
        return (z + nz - 1 - t) % nz if d == 0 else (z + 1 + t) % nz

    def out_part(q, c0, n):
        return dot(gsent[q].T, act[:, c0 : c0 + n])

    def in_part(d, t):
        left = xt[pl.ds(pl.multiple_of(block_of(d, t) * blk, blk), blk), :]
        return dot(left, gpre[:, d * half : (d + 1) * half])

    out_set = (ring_o, osend, orecv)
    in_set = (ring_i, isend, irecv)
    y_set = (ring_y, rysend, ryrecv)

    def pass_on(which, n, d, t, first=False):
        ring = which[0]
        w = n // 2
        for j in (0, 1):
            value = part[d, :, j * w : (j + 1) * w]
            if not first:
                arrived(*which, d, j, t)
                value = value + ring[d, j, t].astype(F32)
            ring[d, j, t] = value.astype(BF)
            hop(*which, d, j, t).start()

    def out_step(t, q):
        for d in (0, 1):
            part[d, :, :zc] = out_part(q[d], d * zc, zc)
        for d in (0, 1):
            pass_on(out_set, zc, d, t, first=isinstance(t, int) and t == 0)

    def in_step(t, ds=(0, 1)):
        for d in ds:
            part[d, :, :half] = in_part(d, t)
        for d in ds:
            pass_on(in_set, half, d, t, first=isinstance(t, int) and t == 0)

    keep = pl.multiple_of(yh * half_rows, half_rows)
    give = pl.multiple_of((1 - yh) * half_rows, half_rows)

    def swap(sbuf, rbuf, ssem, rsem, d, j):
        return pltpu.make_async_remote_copy(
            src_ref=sbuf.at[d, j],
            dst_ref=rbuf.at[d, j],
            send_sem=ssem.at[d, j],
            recv_sem=rsem.at[d, j],
            device_id={"dp": across},
            device_id_type=MESH,
        )

    out_swap = (swap_so, swap_ro, sosend, sorecv)
    in_swap = (swap_si, swap_ri, sisend, sirecv)

    def last_step(which, swapping, fin, n, fill):
        w = n // 2
        for d in (0, 1):
            part[d, :, :n] = fill(d)
        for d in (0, 1):
            for j in (0, 1):
                arrived(*which, d, j, nz - 1)
                cols = slice(j * w, (j + 1) * w)
                part[d, :, cols] = part[d, :, cols] + which[0][d, j, nz - 1].astype(F32)
                swapping[0][d, j] = part[d, pl.ds(give, half_rows), cols].astype(BF)
                swap(*swapping, d, j).start()
                fin[d, j] = part[d, pl.ds(keep, half_rows), cols]

    def finish(swapping, fin, n, out, base):
        w = n // 2
        for d in (0, 1):
            for j in (0, 1):
                swap(*swapping, d, j).wait()
                c0 = base + d * n + j * w
                out[:, c0 : c0 + w] = (fin[d, j] + swapping[1][d, j].astype(F32)).astype(BF)

    def across_copy(d, t):
        return pltpu.make_async_remote_copy(
            src_ref=ysend.at[d, t],
            dst_ref=yrecv.at[d, t],
            send_sem=xsend.at[d, t],
            recv_sem=xrecv.at[d, t],
            device_id={"dp": across},
            device_id_type=MESH,
        )

    def y_part(t, q):
        for d in (0, 1):
            part[d, :, :yc] = out_part(q[d], 2 * zc + d * yc, yc)
            ysend[d, t] = part[d, pl.ds(give, half_rows), :yc].astype(BF)
            across_copy(d, t).start()
            ykeep[d, t] = part[d, pl.ds(keep, half_rows), :yc]

    def y_step(t, first=False, last=False):
        w = yc // 2
        for d in (0, 1):
            across_copy(d, t).wait_recv()
            for j in (0, 1):
                cols = slice(j * w, (j + 1) * w)
                value = ykeep[d, t, :, cols] + yrecv[d, t, :, cols].astype(F32)
                if not first:
                    arrived(*y_set, d, j, t)
                    value = value + ring_y[d, j, t].astype(F32)
                if last:
                    c0 = 2 * zc + d * yc + j * w
                    gout[:, c0 : c0 + w] = value.astype(BF)
                else:
                    ring_y[d, j, t] = value.astype(BF)
                    hop(*y_set, d, j, t).start()

    def both(t):
        return (order(0, t), order(1, t))

    loads[2].wait()
    recv_all(0, stok, taken)
    first_tiles = 2 * zc // tile
    lax.fori_loop(0, first_tiles, forward, 0)
    recv_grads(0)
    out_step(0, both(0))
    lax.fori_loop(first_tiles, hidden // tile, forward, 0)
    y_part(0, both(0))
    recv_grads(1)
    out_step(1, both(1))
    y_part(1, both(1))
    loads[3].wait()
    xt[...] = taken[...].T
    lax.fori_loop(0, width // wtile // 2, out_proj, 0)
    recv_grads(2)
    out_step(2, both(2))
    y_part(2, both(2))
    lax.fori_loop(width // wtile // 2, width // wtile, out_proj, 0)
    recv_grads(3)
    for q in range(nz):
        gflat[:, lane_block(block_at(q))] = gsent[q]
    out_step(3, both(3))
    lax.fori_loop(0, hidden // tile // 2, backward, 0)
    in_step(0, (0,))
    lax.fori_loop(hidden // tile // 2, hidden // tile, backward, 0)
    in_step(0, (1,))
    y_part(3, both(3))

    def y_late(t, c):
        y_part(t, (late(0, t), late(1, t)))
        return c

    lax.fori_loop(4, nz - 1, y_late, 0)
    y_part(nz - 1, both(nz - 1))
    out_step(4, both(4))
    send_all(1, eout, rout)
    lax.fori_loop(0, width // wtile, grad_tokens, 0)
    in_step(1)
    send_all(2, gtak, rgrad)

    def middle(t, c):
        out_step(t, (late(0, t), late(1, t)))
        in_step(t - 3)
        return c

    lax.fori_loop(5, nz - 1, middle, 0)
    last_step(out_set, out_swap, fin_o, zc, lambda d: out_part(nz - 1, d * zc, zc))
    y_step(0, first=True)
    in_step(4)

    def steady(t, c):
        y_step(t)
        in_step(t + 4)
        return c

    lax.fori_loop(1, nz - 5, steady, 0)

    finish(out_swap, fin_o, zc, gout, 0)
    recv_all(1, eout, rout)
    selt = lax.broadcasted_iota(jnp.int32, (tokens, rows), 0).astype(F32) == pick_row
    hi = gate_row.astype(BF).astype(F32)
    mixed[...] = (
        dot(jnp.where(selt, hi, 0.0).astype(BF), rout[...])
        + dot(jnp.where(selt, gate_row - hi, 0.0).astype(BF), rout[...])
    ).astype(BF)
    recv_all(2, gtak, rgrad)
    tgrad[...] = dot(selt.astype(F32).astype(BF), rgrad[...]).astype(BF)

    y_step(3)
    last_step(in_set, in_swap, fin_i, half, lambda d: in_part(d, nz - 1))

    def tail(t, c):
        y_step(t)
        return c

    lax.fori_loop(4, nz - 1, tail, 0)
    finish(in_swap, fin_i, half, gin, 0)
    y_step(nz - 1, last=True)

    for which, src, dst in ((0, stok, taken), (1, eout, rout), (2, gtak, rgrad)):
        sent_all(which, src, dst)

    def grads_gone(i, c):
        def body(k, c):
            grad_chunk(i, (me + k) % n_ex, me).wait_send()
            return c

        lax.fori_loop(1, n_ex, body, 0)
        return c

    lax.fori_loop(0, nz // 2, grads_gone, 0)

    def ring_sent(t, c):
        for d in (0, 1):
            for j in (0, 1):
                for which in (out_set, in_set, y_set):
                    hop(*which, d, j, t).wait_send()
        return c

    lax.fori_loop(0, nz - 1, ring_sent, 0)

    def across_sent(t, c):
        for d in (0, 1):
            across_copy(d, t).wait_send()
        return c

    lax.fori_loop(0, nz, across_sent, 0)


def deliver(*refs):
    sem = refs[-1]
    count = len(refs) // 2
    copies = [
        pltpu.make_async_copy(refs[i], refs[count + i], sem.at[i]) for i in range(count)
    ]
    for copy in copies:
        copy.start()
    for copy in copies:
        copy.wait()


def on_device(n_dp, n_ex, tokens, picks, gates, w_in, w_out, cotangent):
    count, width = tokens.shape
    hidden = w_in.shape[2]
    per = picks.shape[2]
    rows = n_ex * per
    nz = n_dp // 2
    blk = width // nz
    half = hidden // 2
    zc = half * ZC // 8
    yc = half - zc
    vmem = pl.BlockSpec(memory_space=pltpu.VMEM)
    hbm = pl.BlockSpec(memory_space=pl.ANY)
    dma = pltpu.SemaphoreType.DMA
    results = pl.pallas_call(
        functools.partial(kernel, n_dp, n_ex, zc),
        out_shape=(
            jax.ShapeDtypeStruct((count, width), BF),
            jax.ShapeDtypeStruct((count, width), BF),
            jax.ShapeDtypeStruct((width // n_dp, hidden), BF),
            jax.ShapeDtypeStruct((width // n_dp, hidden), BF),
        ),
        in_specs=[hbm, vmem, vmem, hbm, hbm, hbm],
        out_specs=(vmem, vmem, vmem, vmem),
        scratch_shapes=[
            pltpu.VMEM((width, hidden), BF),
            pltpu.VMEM((hidden, width), BF),
            pltpu.VMEM((count, width), BF),
            pltpu.VMEM((count, width), BF),
            pltpu.VMEM((rows, width), BF),
            pltpu.VMEM((nz, rows, blk), BF),
            pltpu.VMEM((rows, width), BF),
            pltpu.VMEM((nz, rows, blk), BF),
            pltpu.VMEM((rows, width), BF),
            pltpu.VMEM((rows, hidden), BF),
            pltpu.VMEM((rows, hidden), F32),
            pltpu.VMEM((rows, hidden), BF),
            pltpu.VMEM((rows, width), BF),
            pltpu.VMEM((rows, width), BF),
            pltpu.VMEM((rows, width), BF),
            pltpu.VMEM((rows, width), BF),
            pltpu.VMEM((width, rows), BF),
            pltpu.VMEM((2, blk, half), F32),
            pltpu.VMEM((2, 2, nz, blk, zc // 2), BF),
            pltpu.VMEM((2, 2, nz, blk, half // 2), BF),
            pltpu.VMEM((2, 2, nz, blk // 2, yc // 2), BF),
            pltpu.VMEM((2, nz, blk // 2, yc), F32),
            pltpu.VMEM((2, nz, blk // 2, yc), BF),
            pltpu.VMEM((2, nz, blk // 2, yc), BF),
            pltpu.VMEM((2, 2, blk // 2, zc // 2), F32),
            pltpu.VMEM((2, 2, blk // 2, half // 2), F32),
            pltpu.VMEM((2, 2, blk // 2, zc // 2), BF),
            pltpu.VMEM((2, 2, blk // 2, zc // 2), BF),
            pltpu.VMEM((2, 2, blk // 2, half // 2), BF),
            pltpu.VMEM((2, 2, blk // 2, half // 2), BF),
            dma((4,)),
            dma((3, n_ex)),
            dma((3, n_ex)),
            dma((nz // 2, n_ex)),
            dma((nz // 2, n_ex)),
            dma((2, 2, nz)),
            dma((2, 2, nz)),
            dma((2, 2, nz)),
            dma((2, 2, nz)),
            dma((2, 2, nz)),
            dma((2, 2, nz)),
            dma((2, nz)),
            dma((2, nz)),
            dma((2, 2)),
            dma((2, 2)),
            dma((2, 2)),
            dma((2, 2)),
        ],
        compiler_params=pltpu.CompilerParams(
            collective_id=0, has_side_effects=True, vmem_limit_bytes=58 * 1024 * 1024
        ),
        cost_estimate=pl.CostEstimate(
            flops=12 * rows * width * hidden,
            bytes_accessed=4 * width * hidden + 8 * count * width,
            transcendentals=2 * rows * hidden,
        ),
    )(tokens, picks, gates, w_in, w_out, cotangent)
    mixed, tgrad, gin, gout = pl.pallas_call(
        deliver,
        out_shape=tuple(jax.ShapeDtypeStruct(a.shape, a.dtype) for a in results),
        in_specs=[vmem] * 4,
        out_specs=(hbm,) * 4,
        scratch_shapes=[dma((4,))],
        compiler_params=pltpu.CompilerParams(vmem_limit_bytes=58 * 1024 * 1024),
    )(*results)
    return mixed, tgrad, gin[:, None, :], gout[:, None, :]


def solution(mesh):
    n_dp, n_ex = mesh.shape["dp"], mesh.shape["expert"]
    in_specs = (
        P(("dp", "expert"), None),
        P(("dp", "expert"), None, None),
        P(("dp", "expert"), None, None),
        P("expert", None, None),
        P("expert", None, None),
        P(("dp", "expert"), None),
    )
    out_specs = (
        P(("dp", "expert"), None),
        P(("dp", "expert"), None),
        P("dp", "expert", None),
        P("dp", "expert", None),
    )
    return jax.shard_map(
        functools.partial(on_device, n_dp, n_ex),
        mesh=mesh,
        in_specs=in_specs,
        out_specs=out_specs,
        check_vma=False,
    )
```

```python
import functools

import jax
import jax.numpy as jnp
from jax import lax
from jax.experimental import pallas as pl
from jax.experimental.pallas import tpu as pltpu
from jax.sharding import PartitionSpec as P

MESH = pl.DeviceIdType.MESH
BF = jnp.bfloat16
F32 = jnp.float32
NT = (((1,), (1,)), ((), ()))
ZC = 4
SUBS = (2, 2, 1)


def dot(a, b):
    return jnp.dot(a, b, preferred_element_type=F32)


def dot_nt(a, b):
    return lax.dot_general(a, b, NT, preferred_element_type=F32)


def kernel(
    n_dp, n_ex, zc,
    tok_hbm, pick, gate, win_hbm, wout_hbm, cot_hbm,
    mixed, tgrad, gin, gout,
    win, wout, tok, cot, stok, sgrad, taken, gsent, gflat, act, dgel, gpre, eout, gtak, rout, rgrad,
    xt, part, ring_o, ring_i, ring_y, ykeep, ysend, yrecv,
    fin_o, fin_i, swap_so, swap_ro, swap_si, swap_ri,
    wsem, tsend, trecv, gsend, grecv,
    osend, orecv, isend, irecv, rysend, ryrecv, xsend, xrecv,
    sosend, sorecv, sisend, sirecv,
):
    nz = n_dp // 2
    tokens, width = tok.shape
    per = pick.shape[2]
    rows = n_ex * per
    hidden = win.shape[1]
    blk = width // nz
    half_rows = blk // 2
    half = hidden // 2
    yc = half - zc
    r = lax.axis_index("dp")
    me = lax.axis_index("expert")
    z = r // 2
    yh = r % 2
    up = (r + 2) % n_dp
    down = (r + n_dp - 2) % n_dp
    across = r + 1 - 2 * yh

    loads = [
        pltpu.make_async_copy(src, dst, wsem.at[i])
        for i, (src, dst) in enumerate(
            ((tok_hbm, tok), (cot_hbm, cot), (win_hbm.at[0], win), (wout_hbm.at[0], wout))
        )
    ]
    for load in loads:
        load.start()

    barrier = pltpu.get_barrier_semaphore()

    def greet(k, c):
        pl.semaphore_signal(
            barrier, inc=1, device_id={"expert": (me + k) % n_ex}, device_id_type=MESH
        )
        return c

    lax.fori_loop(1, n_ex, greet, 0)
    for other in (up, down, across):
        pl.semaphore_signal(barrier, inc=1, device_id={"dp": other}, device_id_type=MESH)

    p2 = pick[0].astype(F32).astype(BF)
    g = gate[0]
    g1 = g.astype(BF)
    g2 = (g - g1.astype(F32)).astype(BF)
    g3 = (g - g1.astype(F32) - g2.astype(F32)).astype(BF)
    row_e = lax.broadcasted_iota(jnp.int32, (rows, n_ex), 0) // per
    expert_of = (row_e == lax.broadcasted_iota(jnp.int32, (rows, n_ex), 1)).astype(F32).astype(BF)
    place = lax.broadcasted_iota(jnp.int32, (rows, per), 0) % per
    here = place == lax.broadcasted_iota(jnp.int32, (rows, per), 1)

    def column(values):
        return jnp.sum(jnp.where(here, values, 0.0), axis=1, keepdims=True)

    pick_col = column(dot(expert_of, p2))
    lanes = lax.broadcasted_iota(jnp.int32, (rows, tokens), 1).astype(F32)
    sel = (lanes == pick_col).astype(F32).astype(BF)
    loads[0].wait()
    stok[...] = dot(sel, tok[...]).astype(BF)

    def block_at(q):
        if q == nz - 1:
            return z
        back = (q + 1) // 2
        return (z + nz // 2 - back) % nz if q % 2 else (z + nz // 2 + back) % nz

    def place_of(d, p):
        return 0 if p == 0 else 2 * p - 1 + d

    def lane_block(b):
        return pl.ds(pl.multiple_of(b * blk, blk), blk)

    pl.semaphore_wait(barrier, n_ex + 2)

    def exchange(which, src, dst, peer, slot):
        return pltpu.make_async_remote_copy(
            src_ref=src.at[pl.ds(peer * per, per)],
            dst_ref=dst.at[pl.ds(slot * per, per)],
            send_sem=tsend.at[which, peer],
            recv_sem=trecv.at[which, slot],
            device_id={"expert": peer},
            device_id_type=MESH,
        )

    def peer_of(i):
        return (me + n_ex // 2 + (1 + i // 2) * (1 - 2 * (i % 2)) + n_ex) % n_ex

    def send_all(which, src, dst):
        exchange(which, src, dst, (me + n_ex // 2) % n_ex, me).start()

        def body(i, c):
            exchange(which, src, dst, peer_of(i), me).start()
            return c

        lax.fori_loop(0, n_ex - 2, body, 0)
        own = pl.ds(me * per, per)
        dst[own, :] = src[own, :]

    def recv_all(which, src, dst):
        def body(k, c):
            peer = (me + k) % n_ex
            exchange(which, src, dst, peer, peer).wait_recv()
            return c

        lax.fori_loop(1, n_ex, body, 0)

    def sent_all(which, src, dst):
        def body(k, c):
            exchange(which, src, dst, (me + k) % n_ex, me).wait_send()
            return c

        lax.fori_loop(1, n_ex, body, 0)

    chunks = ((0, 1), (1, 2), (3, 2), (5, 3))

    def grad_chunk(i, peer, slot):
        at = pl.ds(*chunks[i])
        return pltpu.make_async_remote_copy(
            src_ref=sgrad.at[at, pl.ds(peer * per, per)],
            dst_ref=gsent.at[at, pl.ds(slot * per, per)],
            send_sem=gsend.at[i, peer],
            recv_sem=grecv.at[i, slot],
            device_id={"expert": peer},
            device_id_type=MESH,
        )

    def send_grads(i):
        grad_chunk(i, (me + n_ex // 2) % n_ex, me).start()

        def body(k, c):
            grad_chunk(i, peer_of(k), me).start()
            return c

        lax.fori_loop(0, n_ex - 2, body, 0)

    def recv_grads(i):
        def body(k, c):
            peer = (me + k) % n_ex
            grad_chunk(i, peer, peer).wait_recv()
            return c

        lax.fori_loop(1, n_ex, body, 0)

    send_all(0, stok, taken)
    gate_col = column(dot(expert_of, g1) + dot(expert_of, g2) + dot(expert_of, g3))
    loads[1].wait()
    for q in range(nz):
        sgrad[q] = (dot(sel, cot[:, lane_block(block_at(q))]) * gate_col).astype(BF)
    for i in range(len(chunks)):
        send_grads(i)
    mine = pl.ds(me * per, per)
    for q in range(nz):
        gsent[q, mine, :] = sgrad[q, mine, :]

    here_bf = here.astype(F32).astype(BF)
    own_e = lax.broadcasted_iota(jnp.int32, (n_ex, rows), 0) == (
        lax.broadcasted_iota(jnp.int32, (n_ex, rows), 1) // per
    )

    def as_row(values):
        return jnp.sum(jnp.where(own_e, values, 0.0), axis=0, keepdims=True)

    pick_row = as_row(dot_nt(p2, here_bf))
    gate_row = as_row(dot_nt(g1, here_bf) + dot_nt(g2, here_bf) + dot_nt(g3, here_bf))

    tile = min(256, hidden)
    wtile = min(256, width)

    def forward(j, c):
        cols = pl.ds(pl.multiple_of(j * tile, tile), tile)
        pre = dot(taken[...], win[:, cols])
        cdf = 0.5 * (1.0 + lax.erf(pre * 0.7071067811865476))
        act[:, cols] = (pre * cdf).astype(BF)
        dgel[:, cols] = cdf + pre * (0.3989422804014327 * jnp.exp(-0.5 * pre * pre))
        return c

    def out_proj(j, c):
        cols = pl.ds(pl.multiple_of(j * wtile, wtile), wtile)
        eout[:, cols] = dot(act[...], wout[:, cols]).astype(BF)
        return c

    def backward(j, c):
        cols = pl.ds(pl.multiple_of(j * tile, tile), tile)
        gact = dot_nt(gflat[...], wout[cols, :])
        gpre[:, cols] = (gact * dgel[:, cols]).astype(BF)
        return c

    def grad_tokens(j, c):
        cols = pl.ds(pl.multiple_of(j * wtile, wtile), wtile)
        gtak[:, cols] = dot_nt(gpre[...], win[cols, :]).astype(BF)
        return c

    chains = ((0, 0, 0), (1, 1, 0), (0, 1, 1), (1, 0, 1))
    hops = nz // 2

    def hop(flow, c, j, t):
        ring, ssem, rsem = flow
        return pltpu.make_async_remote_copy(
            src_ref=ring.at[c, j, t],
            dst_ref=ring.at[c, j, t + 1],
            send_sem=ssem.at[c, j, t],
            recv_sem=rsem.at[c, j, t + 1],
            device_id={"dp": (up, down)[chains[c][1]]},
            device_id_type=MESH,
        )

    def arrived(flow, c, j, t):
        ring, ssem, rsem = flow
        pltpu.make_async_remote_copy(
            src_ref=ring.at[c, j, t],
            dst_ref=ring.at[c, j, t],
            send_sem=ssem.at[c, j, t - 1],
            recv_sem=rsem.at[c, j, t],
            device_id={"dp": (up, down)[chains[c][1]]},
            device_id_type=MESH,
        ).wait_recv()

    out_flow = (ring_o, osend, orecv)
    in_flow = (ring_i, isend, irecv)
    y_flow = (ring_y, rysend, ryrecv)

    def out_part(q, c0, n):
        return dot(gsent[q].T, act[:, c0 : c0 + n])

    def in_part(q, c0, n):
        b = block_at(q)
        left = xt[pl.ds(pl.multiple_of(b * blk, blk), blk), :]
        return dot(left, gpre[:, c0 : c0 + n])

    def pass_on(flow, c, t, values, w):
        ring = flow[0]
        subs = ring.shape[1]
        v = w // subs
        for j in range(subs):
            value = values(slice(j * v, (j + 1) * v))
            if t > 0:
                arrived(flow, c, j, t)
                value = value + ring[c, j, t].astype(F32)
            ring[c, j, t] = value.astype(BF)
            hop(flow, c, j, t).start()

    def z_step(flow, product, w, t, which):
        which = [c for c in which if t < hops - chains[c][2]]
        for c in which:
            h, d, p = chains[c]
            part[c, :, :w] = product(place_of(d, t + p), h * w, w)
        for c in which:
            pass_on(flow, c, t, lambda cols, c=c: part[c, :, cols], w)

    def out_step(t, which=(0, 1, 2, 3)):
        z_step(out_flow, out_part, zc, t, which)

    def in_step(t, which=(0, 1, 2, 3)):
        z_step(in_flow, in_part, half, t, which)

    keep = pl.multiple_of(yh * half_rows, half_rows)
    give = pl.multiple_of((1 - yh) * half_rows, half_rows)

    def swap(swapping, h, j):
        sbuf, rbuf, ssem, rsem = swapping
        return pltpu.make_async_remote_copy(
            src_ref=sbuf.at[h, j],
            dst_ref=rbuf.at[h, j],
            send_sem=ssem.at[h, j],
            recv_sem=rsem.at[h, j],
            device_id={"dp": across},
            device_id_type=MESH,
        )

    out_swap = (swap_so, swap_ro, sosend, sorecv)
    in_swap = (swap_si, swap_ri, sisend, sirecv)

    def both_arrived(flow, h, j):
        long, short = h, 2 + h
        arrived(flow, long, j, hops)
        arrived(flow, short, j, hops - 1)
        ring = flow[0]
        return ring[long, j, hops].astype(F32) + ring[short, j, hops - 1].astype(F32)

    def last_step(flow, product, swapping, fin, w):
        subs = flow[0].shape[1]
        v = w // subs
        for h in (0, 1):
            part[h, :, :w] = product(nz - 1, h * w, w)
        for h in (0, 1):
            for j in range(subs):
                cols = slice(j * v, (j + 1) * v)
                part[h, :, cols] = part[h, :, cols] + both_arrived(flow, h, j)
                swapping[0][h, j] = part[h, pl.ds(give, half_rows), cols].astype(BF)
                swap(swapping, h, j).start()
                fin[h, j] = part[h, pl.ds(keep, half_rows), cols]

    def finish(swapping, fin, w, out):
        subs = fin.shape[1]
        v = w // subs
        for h in (0, 1):
            for j in range(subs):
                swap(swapping, h, j).wait()
                c0 = h * w + j * v
                out[:, c0 : c0 + v] = (fin[h, j] + swapping[1][h, j].astype(F32)).astype(BF)

    def across_copy(q):
        return pltpu.make_async_remote_copy(
            src_ref=ysend.at[q],
            dst_ref=yrecv.at[q],
            send_sem=xsend.at[q],
            recv_sem=xrecv.at[q],
            device_id={"dp": across},
            device_id_type=MESH,
        )

    def y_part(q):
        for h in (0, 1):
            cols = slice(h * yc, (h + 1) * yc)
            part[h, :, :yc] = out_part(q, 2 * zc + h * yc, yc)
            ysend[q, :, cols] = part[h, pl.ds(give, half_rows), :yc].astype(BF)
            ykeep[q, :, cols] = part[h, pl.ds(keep, half_rows), :yc]
        across_copy(q).start()

    def y_sum(q, h, cols):
        at = slice(h * yc + cols.start, h * yc + cols.stop)
        return ykeep[q, :, at] + yrecv[q, :, at].astype(F32)

    def y_step(t):
        for c in (0, 1, 2, 3):
            h, d, p = chains[c]
            if t < hops - p:
                q = place_of(d, t + p)
                if c >= 2 or q == 0 and c == 0:
                    across_copy(q).wait_recv()
                pass_on(y_flow, c, t, lambda cols, q=q, h=h: y_sum(q, h, cols), yc)

    def y_last():
        across_copy(nz - 1).wait_recv()
        subs = ring_y.shape[1]
        v = yc // subs
        for h in (0, 1):
            for j in range(subs):
                value = y_sum(nz - 1, h, slice(j * v, (j + 1) * v)) + both_arrived(y_flow, h, j)
                c0 = 2 * zc + h * yc + j * v
                gout[:, c0 : c0 + v] = value.astype(BF)

    loads[2].wait()
    recv_all(0, stok, taken)
    first_tiles = 2 * zc // tile
    all_tiles = hidden // tile
    lax.fori_loop(0, first_tiles, forward, 0)
    recv_grads(0)
    out_step(0, (0, 1))
    middle_tile = (first_tiles + all_tiles) // 2
    lax.fori_loop(first_tiles, middle_tile, forward, 0)
    recv_grads(1)
    out_step(0, (2, 3))
    lax.fori_loop(middle_tile, all_tiles, forward, 0)
    for q in (0, 1, 2):
        y_part(q)
    out_step(1, (0, 1))
    recv_grads(2)
    out_step(1, (2, 3))
    for q in (3, 4):
        y_part(q)
    loads[3].wait()
    xt[...] = taken[...].T
    out_tiles = width // wtile
    lax.fori_loop(0, out_tiles, out_proj, 0)
    recv_grads(3)
    for q in range(nz):
        gflat[:, lane_block(block_at(q))] = gsent[q]
    out_step(2)
    lax.fori_loop(0, all_tiles // 2, backward, 0)
    in_step(0, (0, 2))
    lax.fori_loop(all_tiles // 2, all_tiles, backward, 0)
    in_step(0, (1, 3))
    for q in (5, 6, 7):
        y_part(q)
    out_step(3)
    send_all(1, eout, rout)
    lax.fori_loop(0, out_tiles, grad_tokens, 0)
    send_all(2, gtak, rgrad)
    in_step(1)
    y_step(0)
    last_step(out_flow, out_part, out_swap, fin_o, zc)
    in_step(2)
    y_step(1)
    in_step(3)

    recv_all(1, eout, rout)
    selt = lax.broadcasted_iota(jnp.int32, (tokens, rows), 0).astype(F32) == pick_row
    hi = gate_row.astype(BF).astype(F32)
    mixed[...] = (
        dot(jnp.where(selt, hi, 0.0).astype(BF), rout[...])
        + dot(jnp.where(selt, gate_row - hi, 0.0).astype(BF), rout[...])
    ).astype(BF)
    recv_all(2, gtak, rgrad)
    tgrad[...] = dot(selt.astype(F32).astype(BF), rgrad[...]).astype(BF)

    y_step(2)
    last_step(in_flow, in_part, in_swap, fin_i, half)
    y_step(3)
    finish(out_swap, fin_o, zc, gout)
    y_last()
    finish(in_swap, fin_i, half, gin)

    for which, src, dst in ((0, stok, taken), (1, eout, rout), (2, gtak, rgrad)):
        sent_all(which, src, dst)

    for i in range(len(chunks)):
        def grads_gone(k, c, i=i):
            grad_chunk(i, (me + k) % n_ex, me).wait_send()
            return c

        lax.fori_loop(1, n_ex, grads_gone, 0)

    for flow in (out_flow, in_flow, y_flow):
        for c in range(len(chains)):
            for j in range(flow[0].shape[1]):
                for t in range(hops - chains[c][2]):
                    hop(flow, c, j, t).wait_send()

    def across_sent(q, c):
        across_copy(q).wait_send()
        return c

    lax.fori_loop(0, nz, across_sent, 0)


def deliver(*refs):
    sem = refs[-1]
    count = len(refs) // 2
    copies = [
        pltpu.make_async_copy(refs[i], refs[count + i], sem.at[i]) for i in range(count)
    ]
    for copy in copies:
        copy.start()
    for copy in copies:
        copy.wait()


def on_device(n_dp, n_ex, tokens, picks, gates, w_in, w_out, cotangent):
    count, width = tokens.shape
    hidden = w_in.shape[2]
    per = picks.shape[2]
    rows = n_ex * per
    nz = n_dp // 2
    blk = width // nz
    half = hidden // 2
    zc = half * ZC // 8
    yc = half - zc
    hops = nz // 2
    vmem = pl.BlockSpec(memory_space=pltpu.VMEM)
    hbm = pl.BlockSpec(memory_space=pl.ANY)
    dma = pltpu.SemaphoreType.DMA
    results = pl.pallas_call(
        functools.partial(kernel, n_dp, n_ex, zc),
        out_shape=(
            jax.ShapeDtypeStruct((count, width), BF),
            jax.ShapeDtypeStruct((count, width), BF),
            jax.ShapeDtypeStruct((width // n_dp, hidden), BF),
            jax.ShapeDtypeStruct((width // n_dp, hidden), BF),
        ),
        in_specs=[hbm, vmem, vmem, hbm, hbm, hbm],
        out_specs=(vmem, vmem, vmem, vmem),
        scratch_shapes=[
            pltpu.VMEM((width, hidden), BF),
            pltpu.VMEM((hidden, width), BF),
            pltpu.VMEM((count, width), BF),
            pltpu.VMEM((count, width), BF),
            pltpu.VMEM((rows, width), BF),
            pltpu.VMEM((nz, rows, blk), BF),
            pltpu.VMEM((rows, width), BF),
            pltpu.VMEM((nz, rows, blk), BF),
            pltpu.VMEM((rows, width), BF),
            pltpu.VMEM((rows, hidden), BF),
            pltpu.VMEM((rows, hidden), F32),
            pltpu.VMEM((rows, hidden), BF),
            pltpu.VMEM((rows, width), BF),
            pltpu.VMEM((rows, width), BF),
            pltpu.VMEM((rows, width), BF),
            pltpu.VMEM((rows, width), BF),
            pltpu.VMEM((width, rows), BF),
            pltpu.VMEM((4, blk, half), F32),
            pltpu.VMEM((4, SUBS[0], hops + 1, blk, zc // SUBS[0]), BF),
            pltpu.VMEM((4, SUBS[1], hops + 1, blk, half // SUBS[1]), BF),
            pltpu.VMEM((4, SUBS[2], hops + 1, blk // 2, yc // SUBS[2]), BF),
            pltpu.VMEM((nz, blk // 2, 2 * yc), F32),
            pltpu.VMEM((nz, blk // 2, 2 * yc), BF),
            pltpu.VMEM((nz, blk // 2, 2 * yc), BF),
            pltpu.VMEM((2, SUBS[0], blk // 2, zc // SUBS[0]), F32),
            pltpu.VMEM((2, SUBS[1], blk // 2, half // SUBS[1]), F32),
            pltpu.VMEM((2, SUBS[0], blk // 2, zc // SUBS[0]), BF),
            pltpu.VMEM((2, SUBS[0], blk // 2, zc // SUBS[0]), BF),
            pltpu.VMEM((2, SUBS[1], blk // 2, half // SUBS[1]), BF),
            pltpu.VMEM((2, SUBS[1], blk // 2, half // SUBS[1]), BF),
            dma((4,)),
            dma((3, n_ex)),
            dma((3, n_ex)),
            dma((4, n_ex)),
            dma((4, n_ex)),
            dma((4, SUBS[0], hops + 1)),
            dma((4, SUBS[0], hops + 1)),
            dma((4, SUBS[1], hops + 1)),
            dma((4, SUBS[1], hops + 1)),
            dma((4, SUBS[2], hops + 1)),
            dma((4, SUBS[2], hops + 1)),
            dma((nz,)),
            dma((nz,)),
            dma((2, SUBS[0])),
            dma((2, SUBS[0])),
            dma((2, SUBS[1])),
            dma((2, SUBS[1])),
        ],
        compiler_params=pltpu.CompilerParams(
            collective_id=0, has_side_effects=True, vmem_limit_bytes=58 * 1024 * 1024
        ),
        cost_estimate=pl.CostEstimate(
            flops=12 * rows * width * hidden,
            bytes_accessed=4 * width * hidden + 8 * count * width,
            transcendentals=2 * rows * hidden,
        ),
    )(tokens, picks, gates, w_in, w_out, cotangent)
    mixed, tgrad, gin, gout = pl.pallas_call(
        deliver,
        out_shape=tuple(jax.ShapeDtypeStruct(a.shape, a.dtype) for a in results),
        in_specs=[vmem] * 4,
        out_specs=(hbm,) * 4,
        scratch_shapes=[dma((4,))],
        compiler_params=pltpu.CompilerParams(vmem_limit_bytes=58 * 1024 * 1024),
    )(*results)
    return mixed, tgrad, gin[:, None, :], gout[:, None, :]


def solution(mesh):
    n_dp, n_ex = mesh.shape["dp"], mesh.shape["expert"]
    in_specs = (
        P(("dp", "expert"), None),
        P(("dp", "expert"), None, None),
        P(("dp", "expert"), None, None),
        P("expert", None, None),
        P("expert", None, None),
        P(("dp", "expert"), None),
    )
    out_specs = (
        P(("dp", "expert"), None),
        P(("dp", "expert"), None),
        P("dp", "expert", None),
        P("dp", "expert", None),
    )
    return jax.shard_map(
        functools.partial(on_device, n_dp, n_ex),
        mesh=mesh,
        in_specs=in_specs,
        out_specs=out_specs,
        check_vma=False,
    )
```

```python
import functools

import jax
import jax.numpy as jnp
from jax import lax
from jax.experimental import pallas as pl
from jax.experimental.pallas import tpu as pltpu
from jax.sharding import PartitionSpec as P

MESH = pl.DeviceIdType.MESH
BF = jnp.bfloat16
F32 = jnp.float32
NT = (((1,), (1,)), ((), ()))
ZC = 4
SUBS = (2, 2, 1)


def dot(a, b):
    return jnp.dot(a, b, preferred_element_type=F32)


def dot_nt(a, b):
    return lax.dot_general(a, b, NT, preferred_element_type=F32)


def kernel(
    n_dp, n_ex, zc,
    tok_hbm, pick, gate, win_hbm, wout_hbm, cot_hbm,
    mixed, tgrad, gin, gout,
    win, wout, tok, cot, stok, sgrad, taken, gsent, gflat, act, dgel, gpre, eout, gtak, rout, rgrad,
    xt, part, ring_o, ring_i, ring_y, ykeep, ysend, yrecv,
    fin_o, fin_i, swap_so, swap_ro, swap_si, swap_ri,
    wsem, tsend, trecv, gsend, grecv,
    osend, orecv, isend, irecv, rysend, ryrecv, xsend, xrecv,
    sosend, sorecv, sisend, sirecv,
):
    nz = n_dp // 2
    tokens, width = tok.shape
    per = pick.shape[2]
    rows = n_ex * per
    hidden = win.shape[1]
    blk = width // nz
    half_rows = blk // 2
    half = hidden // 2
    yc = half - zc
    r = lax.axis_index("dp")
    me = lax.axis_index("expert")
    z = r // 2
    yh = r % 2
    up = (r + 2) % n_dp
    down = (r + n_dp - 2) % n_dp
    across = r + 1 - 2 * yh

    loads = [
        pltpu.make_async_copy(src, dst, wsem.at[i])
        for i, (src, dst) in enumerate(
            ((tok_hbm, tok), (cot_hbm, cot), (win_hbm.at[0], win), (wout_hbm.at[0], wout))
        )
    ]
    for load in loads:
        load.start()

    barrier = pltpu.get_barrier_semaphore()

    def greet(k, c):
        pl.semaphore_signal(
            barrier, inc=1, device_id={"expert": (me + k) % n_ex}, device_id_type=MESH
        )
        return c

    lax.fori_loop(1, n_ex, greet, 0)
    for other in (up, down, across):
        pl.semaphore_signal(barrier, inc=1, device_id={"dp": other}, device_id_type=MESH)

    p2 = pick[0].astype(F32).astype(BF)
    g = gate[0]
    g1 = g.astype(BF)
    g2 = (g - g1.astype(F32)).astype(BF)
    g3 = (g - g1.astype(F32) - g2.astype(F32)).astype(BF)
    row_e = lax.broadcasted_iota(jnp.int32, (rows, n_ex), 0) // per
    expert_of = (row_e == lax.broadcasted_iota(jnp.int32, (rows, n_ex), 1)).astype(F32).astype(BF)
    place = lax.broadcasted_iota(jnp.int32, (rows, per), 0) % per
    here = place == lax.broadcasted_iota(jnp.int32, (rows, per), 1)

    def column(values):
        return jnp.sum(jnp.where(here, values, 0.0), axis=1, keepdims=True)

    pick_col = column(dot(expert_of, p2))
    lanes = lax.broadcasted_iota(jnp.int32, (rows, tokens), 1).astype(F32)
    sel = (lanes == pick_col).astype(F32).astype(BF)
    loads[0].wait()
    stok[...] = dot(sel, tok[...]).astype(BF)

    def block_at(q):
        if q == nz - 1:
            return z
        back = (q + 1) // 2
        return (z + nz // 2 - back) % nz if q % 2 else (z + nz // 2 + back) % nz

    def place_of(d, p):
        return 0 if p == 0 else 2 * p - 1 + d

    def lane_block(b):
        return pl.ds(pl.multiple_of(b * blk, blk), blk)

    pl.semaphore_wait(barrier, n_ex + 2)

    def landed(ref, sem):
        pltpu.make_async_remote_copy(
            src_ref=ref, dst_ref=ref, send_sem=sem, recv_sem=sem,
            device_id={"dp": across}, device_id_type=MESH,
        ).wait_recv()

    def gone(ref, sem):
        pltpu.make_async_remote_copy(
            src_ref=ref, dst_ref=ref, send_sem=sem, recv_sem=sem,
            device_id={"dp": across}, device_id_type=MESH,
        ).wait_send()

    def exchange(which, src, dst, peer):
        return pltpu.make_async_remote_copy(
            src_ref=src.at[pl.ds(peer * per, per)],
            dst_ref=dst.at[pl.ds(me * per, per)],
            send_sem=tsend.at[which],
            recv_sem=trecv.at[which],
            device_id={"expert": peer},
            device_id_type=MESH,
        )

    def peer_of(i):
        return (me + n_ex // 2 + (1 + i // 2) * (1 - 2 * (i % 2)) + n_ex) % n_ex

    others = pl.ds(0, rows - per)

    def send_all(which, src, dst):
        exchange(which, src, dst, (me + n_ex // 2) % n_ex).start()

        def body(i, c):
            exchange(which, src, dst, peer_of(i)).start()
            return c

        lax.fori_loop(0, n_ex - 2, body, 0)
        own = pl.ds(me * per, per)
        dst[own, :] = src[own, :]

    def recv_all(which, dst):
        landed(dst.at[others], trecv.at[which])

    chunks = ((0, 1), (1, 2), (3, 2), (5, 3))

    def grad_chunk(i, peer):
        at = pl.ds(*chunks[i])
        return pltpu.make_async_remote_copy(
            src_ref=sgrad.at[at, pl.ds(peer * per, per)],
            dst_ref=gsent.at[at, pl.ds(me * per, per)],
            send_sem=gsend.at[0],
            recv_sem=grecv.at[i],
            device_id={"expert": peer},
            device_id_type=MESH,
        )

    def send_grads(i):
        grad_chunk(i, (me + n_ex // 2) % n_ex).start()

        def body(k, c):
            grad_chunk(i, peer_of(k)).start()
            return c

        lax.fori_loop(0, n_ex - 2, body, 0)

    def recv_grads(i):
        landed(gsent.at[pl.ds(*chunks[i]), others], grecv.at[i])

    send_all(0, stok, taken)
    gate_col = column(dot(expert_of, g1) + dot(expert_of, g2) + dot(expert_of, g3))
    loads[1].wait()
    for q in range(nz):
        sgrad[q] = (dot(sel, cot[:, lane_block(block_at(q))]) * gate_col).astype(BF)
    for i in range(len(chunks)):
        send_grads(i)
    mine = pl.ds(me * per, per)
    for q in range(nz):
        gsent[q, mine, :] = sgrad[q, mine, :]

    here_bf = here.astype(F32).astype(BF)
    own_e = lax.broadcasted_iota(jnp.int32, (n_ex, rows), 0) == (
        lax.broadcasted_iota(jnp.int32, (n_ex, rows), 1) // per
    )

    def as_row(values):
        return jnp.sum(jnp.where(own_e, values, 0.0), axis=0, keepdims=True)

    pick_row = as_row(dot_nt(p2, here_bf))
    gate_row = as_row(dot_nt(g1, here_bf) + dot_nt(g2, here_bf) + dot_nt(g3, here_bf))

    tile = min(256, hidden)
    wtile = min(256, width)

    def forward(j, c):
        cols = pl.ds(pl.multiple_of(j * tile, tile), tile)
        pre = dot(taken[...], win[:, cols])
        cdf = 0.5 * (1.0 + lax.erf(pre * 0.7071067811865476))
        act[:, cols] = (pre * cdf).astype(BF)
        dgel[:, cols] = cdf + pre * (0.3989422804014327 * jnp.exp(-0.5 * pre * pre))
        return c

    def out_proj(j, c):
        cols = pl.ds(pl.multiple_of(j * wtile, wtile), wtile)
        eout[:, cols] = dot(act[...], wout[:, cols]).astype(BF)
        return c

    def backward(j, c):
        cols = pl.ds(pl.multiple_of(j * tile, tile), tile)
        gact = dot_nt(gflat[...], wout[cols, :])
        gpre[:, cols] = (gact * dgel[:, cols]).astype(BF)
        return c

    def grad_tokens(j, c):
        cols = pl.ds(pl.multiple_of(j * wtile, wtile), wtile)
        gtak[:, cols] = dot_nt(gpre[...], win[cols, :]).astype(BF)
        return c

    chains = ((0, 0, 0), (1, 1, 0), (0, 1, 1), (1, 0, 1))
    hops = nz // 2

    def hop(flow, c, j, t):
        ring, ssem, rsem = flow
        return pltpu.make_async_remote_copy(
            src_ref=ring.at[c, j, t],
            dst_ref=ring.at[c, j, t + 1],
            send_sem=ssem.at[c],
            recv_sem=rsem.at[c, j, t],
            device_id={"dp": (up, down)[chains[c][1]]},
            device_id_type=MESH,
        )

    def arrived(flow, c, j, t):
        landed(flow[0].at[c, j, t], flow[2].at[c, j, t - 1])

    out_flow = (ring_o, osend, orecv)
    in_flow = (ring_i, isend, irecv)
    y_flow = (ring_y, rysend, ryrecv)

    def out_part(q, c0, n):
        return dot(gsent[q].T, act[:, c0 : c0 + n])

    def in_part(q, c0, n):
        b = block_at(q)
        left = xt[pl.ds(pl.multiple_of(b * blk, blk), blk), :]
        return dot(left, gpre[:, c0 : c0 + n])

    def pass_on(flow, c, j, t, value):
        ring = flow[0]
        if t > 0:
            arrived(flow, c, j, t)
            value = value + ring[c, j, t].astype(F32)
        ring[c, j, t] = value.astype(BF)
        hop(flow, c, j, t).start()

    def z_step(flow, product, w, t, which, subs):
        v = w // flow[0].shape[1]
        which = [c for c in which if t < hops - chains[c][2]]
        for c in which:
            h, d, p = chains[c]
            c0, n = subs[0] * v, len(subs) * v
            part[c, :, c0 : c0 + n] = product(place_of(d, t + p), h * w + c0, n)
        for j in subs:
            for c in which:
                pass_on(flow, c, j, t, part[c, :, j * v : (j + 1) * v])

    def out_step(t, which=(0, 1, 2, 3), subs=tuple(range(SUBS[0]))):
        z_step(out_flow, out_part, half, t, which, subs)

    def in_step(t, which=(0, 1, 2, 3), subs=tuple(range(SUBS[1]))):
        z_step(in_flow, in_part, zc, t, which, subs)

    keep = pl.multiple_of(yh * half_rows, half_rows)
    give = pl.multiple_of((1 - yh) * half_rows, half_rows)

    def swap(swapping, h, j):
        sbuf, rbuf, ssem, rsem = swapping
        return pltpu.make_async_remote_copy(
            src_ref=sbuf.at[h, j],
            dst_ref=rbuf.at[h, j],
            send_sem=ssem.at[0],
            recv_sem=rsem.at[h, j],
            device_id={"dp": across},
            device_id_type=MESH,
        )

    out_swap = (swap_so, swap_ro, sosend, sorecv)
    in_swap = (swap_si, swap_ri, sisend, sirecv)

    def both_arrived(flow, h, j):
        long, short = h, 2 + h
        arrived(flow, long, j, hops)
        arrived(flow, short, j, hops - 1)
        ring = flow[0]
        return ring[long, j, hops].astype(F32) + ring[short, j, hops - 1].astype(F32)

    def last_step(flow, product, swapping, fin, w):
        subs = flow[0].shape[1]
        v = w // subs
        for h in (0, 1):
            part[h, :, :w] = product(nz - 1, h * w, w)
        for h in (0, 1):
            for j in range(subs):
                cols = slice(j * v, (j + 1) * v)
                part[h, :, cols] = part[h, :, cols] + both_arrived(flow, h, j)
                swapping[0][h, j] = part[h, pl.ds(give, half_rows), cols].astype(BF)
                swap(swapping, h, j).start()
                fin[h, j] = part[h, pl.ds(keep, half_rows), cols]

    def finish(swapping, fin, w, out):
        subs = fin.shape[1]
        v = w // subs
        for h in (0, 1):
            for j in range(subs):
                swap(swapping, h, j).wait_recv()
                c0 = h * w + j * v
                out[:, c0 : c0 + v] = (fin[h, j] + swapping[1][h, j].astype(F32)).astype(BF)

    def across_copy(q):
        return pltpu.make_async_remote_copy(
            src_ref=ysend.at[q],
            dst_ref=yrecv.at[q],
            send_sem=xsend.at[0],
            recv_sem=xrecv.at[q],
            device_id={"dp": across},
            device_id_type=MESH,
        )

    def y_part(q):
        for h in (0, 1):
            cols = slice(h * yc, (h + 1) * yc)
            part[h, :, :yc] = in_part(q, 2 * zc + h * yc, yc)
            ysend[q, :, cols] = part[h, pl.ds(give, half_rows), :yc].astype(BF)
            ykeep[q, :, cols] = part[h, pl.ds(keep, half_rows), :yc]
        across_copy(q).start()

    def y_sum(q, h, cols):
        at = slice(h * yc + cols.start, h * yc + cols.stop)
        return ykeep[q, :, at] + yrecv[q, :, at].astype(F32)

    def y_step(t):
        for c in (0, 1, 2, 3):
            h, d, p = chains[c]
            if t < hops - p:
                q = place_of(d, t + p)
                if c >= 2 or q == 0 and c == 0:
                    across_copy(q).wait_recv()
                v = yc // ring_y.shape[1]
                for j in range(ring_y.shape[1]):
                    pass_on(y_flow, c, j, t, y_sum(q, h, slice(j * v, (j + 1) * v)))

    def y_last():
        across_copy(nz - 1).wait_recv()
        subs = ring_y.shape[1]
        v = yc // subs
        for h in (0, 1):
            for j in range(subs):
                value = y_sum(nz - 1, h, slice(j * v, (j + 1) * v)) + both_arrived(y_flow, h, j)
                c0 = 2 * zc + h * yc + j * v
                gin[:, c0 : c0 + v] = value.astype(BF)

    all_tiles = hidden // tile
    half_tiles = all_tiles // 2
    sub_tiles = half_tiles // SUBS[0]
    loads[2].wait()
    recv_all(0, taken)
    for j in range(SUBS[0]):
        for h in (0, 1):
            t0 = h * half_tiles + j * sub_tiles
            lax.fori_loop(t0, t0 + sub_tiles, forward, 0)
        if j == 0:
            recv_grads(0)
        out_step(0, (0, 1), (j,))
    recv_grads(1)
    out_step(0, (2, 3))
    xt[...] = taken[...].T
    loads[3].wait()
    out_tiles = width // wtile
    lax.fori_loop(0, out_tiles, out_proj, 0)
    recv_grads(2)
    out_step(1, (0, 1), (0,))
    recv_grads(3)
    for q in range(nz):
        gflat[:, lane_block(block_at(q))] = gsent[q]
    z_tiles = 2 * zc // tile
    lax.fori_loop(z_tiles, all_tiles, backward, 0)
    for j in range(1, SUBS[0]):
        out_step(1, (0, 1), (j,))
    for q in range(nz // 2):
        y_part(q)
    out_step(1, (2, 3))
    for q in range(nz // 2, nz):
        y_part(q)
    lax.fori_loop(0, z_tiles, backward, 0)
    in_step(0)
    send_all(1, eout, rout)
    lax.fori_loop(0, out_tiles, grad_tokens, 0)
    send_all(2, gtak, rgrad)
    out_step(2)
    in_step(1)
    y_step(0)
    out_step(3)
    in_step(2)
    y_step(1)
    in_step(3)
    last_step(out_flow, out_part, out_swap, fin_o, half)

    recv_all(1, rout)
    selt = lax.broadcasted_iota(jnp.int32, (tokens, rows), 0).astype(F32) == pick_row
    hi = gate_row.astype(BF).astype(F32)
    mixed[...] = (
        dot(jnp.where(selt, hi, 0.0).astype(BF), rout[...])
        + dot(jnp.where(selt, gate_row - hi, 0.0).astype(BF), rout[...])
    ).astype(BF)
    recv_all(2, rgrad)
    tgrad[...] = dot(selt.astype(F32).astype(BF), rgrad[...]).astype(BF)

    y_step(2)
    last_step(in_flow, in_part, in_swap, fin_i, zc)
    y_step(3)
    finish(out_swap, fin_o, half, gout)
    y_last()
    finish(in_swap, fin_i, zc, gin)

    for which, src in enumerate((stok, eout, gtak)):
        gone(src.at[others], tsend.at[which])
    gone(sgrad.at[:, others], gsend.at[0])
    for ring, ssem, _ in (out_flow, in_flow, y_flow):
        for c in range(len(chains)):
            gone(ring.at[c, :, pl.ds(0, hops - chains[c][2])], ssem.at[c])
    gone(swap_so, sosend.at[0])
    gone(swap_si, sisend.at[0])
    gone(ysend, xsend.at[0])


def deliver(*refs):
    sem = refs[-1]
    count = len(refs) // 2
    copies = [
        pltpu.make_async_copy(refs[i], refs[count + i], sem.at[i]) for i in range(count)
    ]
    for copy in copies:
        copy.start()
    for copy in copies:
        copy.wait()


def on_device(n_dp, n_ex, tokens, picks, gates, w_in, w_out, cotangent):
    count, width = tokens.shape
    hidden = w_in.shape[2]
    per = picks.shape[2]
    rows = n_ex * per
    nz = n_dp // 2
    blk = width // nz
    half = hidden // 2
    zc = half * ZC // 8
    yc = half - zc
    hops = nz // 2
    vmem = pl.BlockSpec(memory_space=pltpu.VMEM)
    hbm = pl.BlockSpec(memory_space=pl.ANY)
    dma = pltpu.SemaphoreType.DMA
    results = pl.pallas_call(
        functools.partial(kernel, n_dp, n_ex, zc),
        out_shape=(
            jax.ShapeDtypeStruct((count, width), BF),
            jax.ShapeDtypeStruct((count, width), BF),
            jax.ShapeDtypeStruct((width // n_dp, hidden), BF),
            jax.ShapeDtypeStruct((width // n_dp, hidden), BF),
        ),
        in_specs=[hbm, vmem, vmem, hbm, hbm, hbm],
        out_specs=(vmem, vmem, vmem, vmem),
        scratch_shapes=[
            pltpu.VMEM((width, hidden), BF),
            pltpu.VMEM((hidden, width), BF),
            pltpu.VMEM((count, width), BF),
            pltpu.VMEM((count, width), BF),
            pltpu.VMEM((rows, width), BF),
            pltpu.VMEM((nz, rows, blk), BF),
            pltpu.VMEM((rows, width), BF),
            pltpu.VMEM((nz, rows, blk), BF),
            pltpu.VMEM((rows, width), BF),
            pltpu.VMEM((rows, hidden), BF),
            pltpu.VMEM((rows, hidden), F32),
            pltpu.VMEM((rows, hidden), BF),
            pltpu.VMEM((rows, width), BF),
            pltpu.VMEM((rows, width), BF),
            pltpu.VMEM((rows, width), BF),
            pltpu.VMEM((rows, width), BF),
            pltpu.VMEM((width, rows), BF),
            pltpu.VMEM((4, blk, half), F32),
            pltpu.VMEM((4, SUBS[0], hops + 1, blk, half // SUBS[0]), BF),
            pltpu.VMEM((4, SUBS[1], hops + 1, blk, zc // SUBS[1]), BF),
            pltpu.VMEM((4, SUBS[2], hops + 1, blk // 2, yc // SUBS[2]), BF),
            pltpu.VMEM((nz, blk // 2, 2 * yc), F32),
            pltpu.VMEM((nz, blk // 2, 2 * yc), BF),
            pltpu.VMEM((nz, blk // 2, 2 * yc), BF),
            pltpu.VMEM((2, SUBS[0], blk // 2, half // SUBS[0]), F32),
            pltpu.VMEM((2, SUBS[1], blk // 2, zc // SUBS[1]), F32),
            pltpu.VMEM((2, SUBS[0], blk // 2, half // SUBS[0]), BF),
            pltpu.VMEM((2, SUBS[0], blk // 2, half // SUBS[0]), BF),
            pltpu.VMEM((2, SUBS[1], blk // 2, zc // SUBS[1]), BF),
            pltpu.VMEM((2, SUBS[1], blk // 2, zc // SUBS[1]), BF),
            dma((4,)),
            dma((3,)),
            dma((3,)),
            dma((1,)),
            dma((4,)),
            dma((4,)),
            dma((4, SUBS[0], hops)),
            dma((4,)),
            dma((4, SUBS[1], hops)),
            dma((4,)),
            dma((4, SUBS[2], hops)),
            dma((1,)),
            dma((nz,)),
            dma((1,)),
            dma((2, SUBS[0])),
            dma((1,)),
            dma((2, SUBS[1])),
        ],
        compiler_params=pltpu.CompilerParams(
            collective_id=0, has_side_effects=True, vmem_limit_bytes=58 * 1024 * 1024
        ),
        cost_estimate=pl.CostEstimate(
            flops=12 * rows * width * hidden,
            bytes_accessed=4 * width * hidden + 8 * count * width,
            transcendentals=2 * rows * hidden,
        ),
    )(tokens, picks, gates, w_in, w_out, cotangent)
    mixed, tgrad, gin, gout = pl.pallas_call(
        deliver,
        out_shape=tuple(jax.ShapeDtypeStruct(a.shape, a.dtype) for a in results),
        in_specs=[vmem] * 4,
        out_specs=(hbm,) * 4,
        scratch_shapes=[dma((4,))],
        compiler_params=pltpu.CompilerParams(vmem_limit_bytes=58 * 1024 * 1024),
    )(*results)
    return mixed, tgrad, gin[:, None, :], gout[:, None, :]


def solution(mesh):
    n_dp, n_ex = mesh.shape["dp"], mesh.shape["expert"]
    in_specs = (
        P(("dp", "expert"), None),
        P(("dp", "expert"), None, None),
        P(("dp", "expert"), None, None),
        P("expert", None, None),
        P("expert", None, None),
        P(("dp", "expert"), None),
    )
    out_specs = (
        P(("dp", "expert"), None),
        P(("dp", "expert"), None),
        P("dp", "expert", None),
        P("dp", "expert", None),
    )
    return jax.shard_map(
        functools.partial(on_device, n_dp, n_ex),
        mesh=mesh,
        in_specs=in_specs,
        out_specs=out_specs,
        check_vma=False,
    )
```

```python
import functools

import jax
import jax.numpy as jnp
from jax import lax
from jax.experimental import pallas as pl
from jax.experimental.pallas import tpu as pltpu
from jax.sharding import PartitionSpec as P

MESH = pl.DeviceIdType.MESH
BF = jnp.bfloat16
F32 = jnp.float32
NT = (((1,), (1,)), ((), ()))
ZC = 3
SUBS = (4, 3, 1)


def dot(a, b):
    return jnp.dot(a, b, preferred_element_type=F32)


def dot_nt(a, b):
    return lax.dot_general(a, b, NT, preferred_element_type=F32)


def kernel(
    n_dp, n_ex, zc,
    tok_hbm, pick, gate, win_hbm, wout_hbm, cot_hbm,
    mixed_hbm, tgrad_hbm, gin_hbm, gout_hbm,
    mixed, tgrad, gin, gout, win, wout, tok, cot, stok, sgrad, taken, gsent, gflat, act, dgel, gpre, eout, gtak, rout, rgrad,
    xt, part, ring_o, ring_i, ring_y, ykeep, ysend, yrecv,
    fin_o, fin_i, swap_so, swap_ro, swap_si, swap_ri,
    wsem, ressem, tsend, trecv, gsend, grecv,
    osend, orecv, isend, irecv, rysend, ryrecv, xsend, xrecv,
    sosend, sorecv, sisend, sirecv,
):
    nz = n_dp // 2
    tokens, width = tok.shape
    per = pick.shape[2]
    rows = n_ex * per
    hidden = win.shape[1]
    blk = width // nz
    half_rows = blk // 2
    half = hidden // 2
    yc = half - zc
    r = lax.axis_index("dp")
    me = lax.axis_index("expert")
    z = r // 2
    yh = r % 2
    up = (r + 2) % n_dp
    down = (r + n_dp - 2) % n_dp
    across = r + 1 - 2 * yh

    barrier = pltpu.get_barrier_semaphore()

    def greet(k, c):
        pl.semaphore_signal(
            barrier, inc=1, device_id={"expert": (me + k) % n_ex}, device_id_type=MESH
        )
        return c

    lax.fori_loop(1, n_ex, greet, 0)
    for other in (up, down, across):
        pl.semaphore_signal(barrier, inc=1, device_id={"dp": other}, device_id_type=MESH)

    loads = [
        pltpu.make_async_copy(src, dst, wsem.at[i])
        for i, (src, dst) in enumerate(
            ((tok_hbm, tok), (cot_hbm, cot), (win_hbm.at[0], win), (wout_hbm.at[0], wout))
        )
    ]
    for load in loads:
        load.start()

    p2 = pick[0].astype(F32).astype(BF)
    g = gate[0]
    g1 = g.astype(BF)
    g2 = (g - g1.astype(F32)).astype(BF)
    g3 = (g - g1.astype(F32) - g2.astype(F32)).astype(BF)
    row_e = lax.broadcasted_iota(jnp.int32, (n_ex, per, n_ex), 0).reshape(rows, n_ex)
    expert_of = (row_e == lax.broadcasted_iota(jnp.int32, (rows, n_ex), 1)).astype(F32).astype(BF)
    place = lax.broadcasted_iota(jnp.int32, (n_ex, per, per), 1).reshape(rows, per)
    here = place == lax.broadcasted_iota(jnp.int32, (rows, per), 1)

    def column(values):
        return jnp.sum(jnp.where(here, values, 0.0), axis=1, keepdims=True)

    pick_col = column(dot(expert_of, p2))
    lanes = lax.broadcasted_iota(jnp.int32, (rows, tokens), 1).astype(F32)
    sel = (lanes == pick_col).astype(F32).astype(BF)
    loads[0].wait()
    stok[...] = dot(sel, tok[...]).astype(BF)

    def block_at(q):
        if q == nz - 1:
            return z
        back = (q + 1) // 2
        return (z + nz // 2 - back) % nz if q % 2 else (z + nz // 2 + back) % nz

    def place_of(d, p):
        return 0 if p == 0 else 2 * p - 1 + d

    def lane_block(b):
        return pl.ds(pl.multiple_of(b * blk, blk), blk)

    pl.semaphore_wait(barrier, n_ex + 2)

    def landed(ref, sem):
        pltpu.make_async_remote_copy(
            src_ref=ref, dst_ref=ref, send_sem=sem, recv_sem=sem,
            device_id={"dp": across}, device_id_type=MESH,
        ).wait_recv()

    def gone(ref, sem):
        pltpu.make_async_remote_copy(
            src_ref=ref, dst_ref=ref, send_sem=sem, recv_sem=sem,
            device_id={"dp": across}, device_id_type=MESH,
        ).wait_send()

    def exchange(which, src, dst, peer):
        return pltpu.make_async_remote_copy(
            src_ref=src.at[pl.ds(peer * per, per)],
            dst_ref=dst.at[pl.ds(me * per, per)],
            send_sem=tsend.at[which],
            recv_sem=trecv.at[which],
            device_id={"expert": peer},
            device_id_type=MESH,
        )

    def peer_of(i):
        return (me + n_ex // 2 + (1 + i // 2) * (1 - 2 * (i % 2)) + n_ex) % n_ex

    others = pl.ds(0, rows - per)

    def send_all(which, src, dst):
        exchange(which, src, dst, (me + n_ex // 2) % n_ex).start()

        def body(i, c):
            exchange(which, src, dst, peer_of(i)).start()
            return c

        lax.fori_loop(0, n_ex - 2, body, 0)
        own = pl.ds(me * per, per)
        dst[own, :] = src[own, :]

    def recv_all(which, dst):
        landed(dst.at[others], trecv.at[which])

    chunks = ((0, 1), (1, 2), (3, 2), (5, 3))

    def grad_chunk(i, peer):
        at = pl.ds(*chunks[i])
        return pltpu.make_async_remote_copy(
            src_ref=sgrad.at[at, pl.ds(peer * per, per)],
            dst_ref=gsent.at[at, pl.ds(me * per, per)],
            send_sem=gsend.at[0],
            recv_sem=grecv.at[i],
            device_id={"expert": peer},
            device_id_type=MESH,
        )

    def send_grads(i):
        grad_chunk(i, (me + n_ex // 2) % n_ex).start()

        def body(k, c):
            grad_chunk(i, peer_of(k)).start()
            return c

        lax.fori_loop(0, n_ex - 2, body, 0)

    def recv_grads(i):
        landed(gsent.at[pl.ds(*chunks[i]), others], grecv.at[i])

    send_all(0, stok, taken)
    gate_col = column(dot(expert_of, g1) + dot(expert_of, g2) + dot(expert_of, g3))
    loads[1].wait()
    for q in range(nz):
        sgrad[q] = (dot(sel, cot[:, lane_block(block_at(q))]) * gate_col).astype(BF)
    for i in range(len(chunks)):
        send_grads(i)
    mine = pl.ds(me * per, per)
    for q in range(nz):
        gsent[q, mine, :] = sgrad[q, mine, :]

    here_bf = here.astype(F32).astype(BF)
    first = per * lax.broadcasted_iota(jnp.int32, (n_ex, rows), 0)
    at_row = lax.broadcasted_iota(jnp.int32, (n_ex, rows), 1)
    own_e = (at_row >= first) & (at_row < first + per)

    def as_row(values):
        return jnp.sum(jnp.where(own_e, values, 0.0), axis=0, keepdims=True)

    pick_row = as_row(dot_nt(p2, here_bf))
    gate_row = as_row(dot_nt(g1, here_bf) + dot_nt(g2, here_bf) + dot_nt(g3, here_bf))

    tile = min(256, hidden)
    wtile = min(256, width)

    def forward(j, c):
        cols = pl.ds(pl.multiple_of(j * tile, tile), tile)
        pre = dot(taken[...], win[:, cols])
        cdf = 0.5 * (1.0 + lax.erf(pre * 0.7071067811865476))
        act[:, cols] = (pre * cdf).astype(BF)
        dgel[:, cols] = cdf + pre * (0.3989422804014327 * jnp.exp(-0.5 * pre * pre))
        return c

    def out_proj(j, c):
        cols = pl.ds(pl.multiple_of(j * wtile, wtile), wtile)
        eout[:, cols] = dot(act[...], wout[:, cols]).astype(BF)
        return c

    def backward(j, c):
        cols = pl.ds(pl.multiple_of(j * tile, tile), tile)
        gact = dot_nt(gflat[...], wout[cols, :])
        gpre[:, cols] = (gact * dgel[:, cols]).astype(BF)
        return c

    def grad_tokens(j, c):
        cols = pl.ds(pl.multiple_of(j * wtile, wtile), wtile)
        gtak[:, cols] = dot_nt(gpre[...], win[cols, :]).astype(BF)
        return c

    chains = ((0, 0, 0), (1, 1, 0), (0, 1, 1), (1, 0, 1))
    hops = nz // 2

    def hop(flow, c, j, t):
        ring, ssem, rsem = flow
        return pltpu.make_async_remote_copy(
            src_ref=ring.at[c, j, t],
            dst_ref=ring.at[c, j, t + 1],
            send_sem=ssem.at[c],
            recv_sem=rsem.at[c, j, t],
            device_id={"dp": (up, down)[chains[c][1]]},
            device_id_type=MESH,
        )

    def arrived(flow, c, j, t):
        landed(flow[0].at[c, j, t], flow[2].at[c, j, t - 1])

    out_flow = (ring_o, osend, orecv)
    in_flow = (ring_i, isend, irecv)
    y_flow = (ring_y, rysend, ryrecv)

    def out_part(q, c0, n):
        return dot(gsent[q].T, act[:, c0 : c0 + n])

    def in_part(q, c0, n):
        b = block_at(q)
        left = xt[pl.ds(pl.multiple_of(b * blk, blk), blk), :]
        return dot(left, gpre[:, c0 : c0 + n])

    def pass_on(flow, c, j, t, value):
        ring = flow[0]
        if t > 0:
            arrived(flow, c, j, t)
            value = value + ring[c, j, t].astype(F32)
        ring[c, j, t] = value.astype(BF)
        hop(flow, c, j, t).start()

    def z_step(flow, product, w, t, which, subs):
        v = w // flow[0].shape[1]
        which = [c for c in which if t < hops - chains[c][2]]
        for c in which:
            h, d, p = chains[c]
            c0, n = subs[0] * v, len(subs) * v
            part[c, :, c0 : c0 + n] = product(place_of(d, t + p), h * w + c0, n)
        for j in subs:
            for c in which:
                pass_on(flow, c, j, t, part[c, :, j * v : (j + 1) * v])

    def out_step(t, which=(0, 1, 2, 3), subs=tuple(range(SUBS[0]))):
        z_step(out_flow, out_part, half, t, which, subs)

    def in_step(t, which=(0, 1, 2, 3), subs=tuple(range(SUBS[1]))):
        z_step(in_flow, in_part, zc, t, which, subs)

    keep = pl.multiple_of(yh * half_rows, half_rows)
    give = pl.multiple_of((1 - yh) * half_rows, half_rows)

    def swap(swapping, h, j):
        sbuf, rbuf, ssem, rsem = swapping
        return pltpu.make_async_remote_copy(
            src_ref=sbuf.at[h, j],
            dst_ref=rbuf.at[h, j],
            send_sem=ssem.at[0],
            recv_sem=rsem.at[h, j],
            device_id={"dp": across},
            device_id_type=MESH,
        )

    out_swap = (swap_so, swap_ro, sosend, sorecv)
    in_swap = (swap_si, swap_ri, sisend, sirecv)

    def both_arrived(flow, h, j):
        long, short = h, 2 + h
        arrived(flow, long, j, hops)
        arrived(flow, short, j, hops - 1)
        ring = flow[0]
        return ring[long, j, hops].astype(F32) + ring[short, j, hops - 1].astype(F32)

    def last_step(flow, product, swapping, fin, w):
        subs = flow[0].shape[1]
        v = w // subs
        for h in (0, 1):
            part[h, :, :w] = product(nz - 1, h * w, w)
        for h in (0, 1):
            for j in range(subs):
                cols = slice(j * v, (j + 1) * v)
                part[h, :, cols] = part[h, :, cols] + both_arrived(flow, h, j)
                swapping[0][h, j] = part[h, pl.ds(give, half_rows), cols].astype(BF)
                swap(swapping, h, j).start()
                fin[h, j] = part[h, pl.ds(keep, half_rows), cols]

    def finish(swapping, fin, w, out):
        subs = fin.shape[1]
        v = w // subs
        for h in (0, 1):
            for j in range(subs):
                swap(swapping, h, j).wait_recv()
                c0 = h * w + j * v
                out[:, c0 : c0 + v] = (fin[h, j] + swapping[1][h, j].astype(F32)).astype(BF)

    def across_copy(q):
        return pltpu.make_async_remote_copy(
            src_ref=ysend.at[q],
            dst_ref=yrecv.at[q],
            send_sem=xsend.at[0],
            recv_sem=xrecv.at[q],
            device_id={"dp": across},
            device_id_type=MESH,
        )

    def y_part(q):
        for h in (0, 1):
            cols = slice(h * yc, (h + 1) * yc)
            part[h, :, :yc] = in_part(q, 2 * zc + h * yc, yc)
            ysend[q, :, cols] = part[h, pl.ds(give, half_rows), :yc].astype(BF)
            ykeep[q, :, cols] = part[h, pl.ds(keep, half_rows), :yc]
        across_copy(q).start()

    def y_sum(q, h, cols):
        at = slice(h * yc + cols.start, h * yc + cols.stop)
        return ykeep[q, :, at] + yrecv[q, :, at].astype(F32)

    def y_step(t):
        for c in (0, 1, 2, 3):
            h, d, p = chains[c]
            if t < hops - p:
                q = place_of(d, t + p)
                if c >= 2 or q == 0 and c == 0:
                    across_copy(q).wait_recv()
                v = yc // ring_y.shape[1]
                for j in range(ring_y.shape[1]):
                    pass_on(y_flow, c, j, t, y_sum(q, h, slice(j * v, (j + 1) * v)))

    def y_last():
        across_copy(nz - 1).wait_recv()
        subs = ring_y.shape[1]
        v = yc // subs
        for h in (0, 1):
            for j in range(subs):
                value = y_sum(nz - 1, h, slice(j * v, (j + 1) * v)) + both_arrived(y_flow, h, j)
                c0 = 2 * zc + h * yc + j * v
                gin[:, c0 : c0 + v] = value.astype(BF)

    all_tiles = hidden // tile
    half_tiles = all_tiles // 2
    sub_tiles = half_tiles // SUBS[0]
    loads[2].wait()
    recv_all(0, taken)
    for j in range(SUBS[0]):
        for h in (0, 1):
            t0 = h * half_tiles + j * sub_tiles
            lax.fori_loop(t0, t0 + sub_tiles, forward, 0)
        if j == 0:
            recv_grads(0)
        out_step(0, (0, 1), (j,))
    recv_grads(1)
    out_step(0, (2, 3))
    xt[...] = taken[...].T
    loads[3].wait()
    out_tiles = width // wtile
    lax.fori_loop(0, out_tiles, out_proj, 0)
    recv_grads(2)
    out_step(1, (0, 1), (0,))
    recv_grads(3)
    send_all(1, eout, rout)
    for q in range(nz):
        gflat[:, lane_block(block_at(q))] = gsent[q]
    z_tiles = 2 * zc // tile
    lax.fori_loop(z_tiles, all_tiles, backward, 0)
    for j in range(1, SUBS[0]):
        out_step(1, (0, 1), (j,))
    for q in range(nz // 2):
        y_part(q)
    out_step(1, (2, 3))
    for q in range(nz // 2, nz):
        y_part(q)
    lax.fori_loop(0, z_tiles, backward, 0)
    in_step(0)
    lax.fori_loop(0, out_tiles, grad_tokens, 0)
    send_all(2, gtak, rgrad)
    out_step(2)
    in_step(1)
    y_step(0)
    out_step(3)
    in_step(2)
    y_step(1)
    in_step(3)
    last_step(out_flow, out_part, out_swap, fin_o, half)

    def store(i, src, dst):
        return pltpu.make_async_copy(src, dst, ressem.at[i])

    recv_all(1, rout)
    selt = lax.broadcasted_iota(jnp.int32, (tokens, rows), 0).astype(F32) == pick_row
    hi = gate_row.astype(BF).astype(F32)
    mixed[...] = (
        dot(jnp.where(selt, hi, 0.0).astype(BF), rout[...])
        + dot(jnp.where(selt, gate_row - hi, 0.0).astype(BF), rout[...])
    ).astype(BF)
    store(0, mixed, mixed_hbm).start()
    recv_all(2, rgrad)
    tgrad[...] = dot(selt.astype(F32).astype(BF), rgrad[...]).astype(BF)
    store(1, tgrad, tgrad_hbm).start()

    y_step(2)
    last_step(in_flow, in_part, in_swap, fin_i, zc)
    y_step(3)
    finish(out_swap, fin_o, half, gout)
    store(2, gout, gout_hbm).start()
    y_last()
    finish(in_swap, fin_i, zc, gin)
    store(3, gin, gin_hbm).start()

    for which, src in enumerate((stok, eout, gtak)):
        gone(src.at[others], tsend.at[which])
    gone(sgrad.at[:, others], gsend.at[0])
    for ring, ssem, _ in (out_flow, in_flow, y_flow):
        for c in range(len(chains)):
            gone(ring.at[c, :, pl.ds(0, hops - chains[c][2])], ssem.at[c])
    gone(swap_so, sosend.at[0])
    gone(swap_si, sisend.at[0])
    gone(ysend, xsend.at[0])
    store(0, mixed, mixed_hbm).wait()
    store(1, tgrad, tgrad_hbm).wait()
    store(2, gout, gout_hbm).wait()
    store(3, gin, gin_hbm).wait()


def deliver(*refs):
    count = len(refs) // 3
    source, target, held = (refs[i * count : (i + 1) * count] for i in range(3))
    loaded, stored = refs[3 * count :]
    loads = [pltpu.make_async_copy(source[i], held[i], loaded.at[i]) for i in range(count)]
    stores = [pltpu.make_async_copy(held[i], target[i], stored.at[i]) for i in range(count)]
    for load in loads:
        load.start()
    for load, store in zip(loads, stores):
        load.wait()
        store.start()
    for store in stores:
        store.wait()


def on_device(n_dp, n_ex, tokens, picks, gates, w_in, w_out, cotangent):
    count, width = tokens.shape
    hidden = w_in.shape[2]
    per = picks.shape[2]
    rows = n_ex * per
    nz = n_dp // 2
    blk = width // nz
    half = hidden // 2
    zc = half * ZC // 8
    yc = half - zc
    hops = nz // 2
    vmem = pl.BlockSpec(memory_space=pltpu.VMEM)
    hbm = pl.BlockSpec(memory_space=pl.ANY)
    dma = pltpu.SemaphoreType.DMA
    results = pl.pallas_call(
        functools.partial(kernel, n_dp, n_ex, zc),
        out_shape=(
            jax.ShapeDtypeStruct((count, width), BF),
            jax.ShapeDtypeStruct((count, width), BF),
            jax.ShapeDtypeStruct((width // n_dp, hidden), BF),
            jax.ShapeDtypeStruct((width // n_dp, hidden), BF),
        ),
        in_specs=[hbm, vmem, vmem, hbm, hbm, hbm],
        out_specs=(hbm, hbm, hbm, hbm),
        scratch_shapes=[
            pltpu.VMEM((count, width), BF),
            pltpu.VMEM((count, width), BF),
            pltpu.VMEM((width // n_dp, hidden), BF),
            pltpu.VMEM((width // n_dp, hidden), BF),
            pltpu.VMEM((width, hidden), BF),
            pltpu.VMEM((hidden, width), BF),
            pltpu.VMEM((count, width), BF),
            pltpu.VMEM((count, width), BF),
            pltpu.VMEM((rows, width), BF),
            pltpu.VMEM((nz, rows, blk), BF),
            pltpu.VMEM((rows, width), BF),
            pltpu.VMEM((nz, rows, blk), BF),
            pltpu.VMEM((rows, width), BF),
            pltpu.VMEM((rows, hidden), BF),
            pltpu.VMEM((rows, hidden), F32),
            pltpu.VMEM((rows, hidden), BF),
            pltpu.VMEM((rows, width), BF),
            pltpu.VMEM((rows, width), BF),
            pltpu.VMEM((rows, width), BF),
            pltpu.VMEM((rows, width), BF),
            pltpu.VMEM((width, rows), BF),
            pltpu.VMEM((4, blk, half), F32),
            pltpu.VMEM((4, SUBS[0], hops + 1, blk, half // SUBS[0]), BF),
            pltpu.VMEM((4, SUBS[1], hops + 1, blk, zc // SUBS[1]), BF),
            pltpu.VMEM((4, SUBS[2], hops + 1, blk // 2, yc // SUBS[2]), BF),
            pltpu.VMEM((nz, blk // 2, 2 * yc), F32),
            pltpu.VMEM((nz, blk // 2, 2 * yc), BF),
            pltpu.VMEM((nz, blk // 2, 2 * yc), BF),
            pltpu.VMEM((2, SUBS[0], blk // 2, half // SUBS[0]), F32),
            pltpu.VMEM((2, SUBS[1], blk // 2, zc // SUBS[1]), F32),
            pltpu.VMEM((2, SUBS[0], blk // 2, half // SUBS[0]), BF),
            pltpu.VMEM((2, SUBS[0], blk // 2, half // SUBS[0]), BF),
            pltpu.VMEM((2, SUBS[1], blk // 2, zc // SUBS[1]), BF),
            pltpu.VMEM((2, SUBS[1], blk // 2, zc // SUBS[1]), BF),
            dma((4,)),
            dma((4,)),
            dma((3,)),
            dma((3,)),
            dma((1,)),
            dma((4,)),
            dma((4,)),
            dma((4, SUBS[0], hops)),
            dma((4,)),
            dma((4, SUBS[1], hops)),
            dma((4,)),
            dma((4, SUBS[2], hops)),
            dma((1,)),
            dma((nz,)),
            dma((1,)),
            dma((2, SUBS[0])),
            dma((1,)),
            dma((2, SUBS[1])),
        ],
        compiler_params=pltpu.CompilerParams(
            collective_id=0, has_side_effects=True, vmem_limit_bytes=58 * 1024 * 1024
        ),
        cost_estimate=pl.CostEstimate(
            flops=12 * rows * width * hidden,
            bytes_accessed=4 * width * hidden + 8 * count * width,
            transcendentals=2 * rows * hidden,
        ),
    )(tokens, picks, gates, w_in, w_out, cotangent)
    mixed, tgrad, gin, gout = pl.pallas_call(
        deliver,
        out_shape=tuple(jax.ShapeDtypeStruct(a.shape, a.dtype) for a in results),
        in_specs=[hbm] * 4,
        out_specs=(hbm,) * 4,
        scratch_shapes=[pltpu.VMEM(a.shape, a.dtype) for a in results] + [dma((4,)), dma((4,))],
        compiler_params=pltpu.CompilerParams(vmem_limit_bytes=58 * 1024 * 1024),
    )(*results)
    return mixed, tgrad, gin[:, None, :], gout[:, None, :]


def solution(mesh):
    n_dp, n_ex = mesh.shape["dp"], mesh.shape["expert"]
    in_specs = (
        P(("dp", "expert"), None),
        P(("dp", "expert"), None, None),
        P(("dp", "expert"), None, None),
        P("expert", None, None),
        P("expert", None, None),
        P(("dp", "expert"), None),
    )
    out_specs = (
        P(("dp", "expert"), None),
        P(("dp", "expert"), None),
        P("dp", "expert", None),
        P("dp", "expert", None),
    )
    return jax.shard_map(
        functools.partial(on_device, n_dp, n_ex),
        mesh=mesh,
        in_specs=in_specs,
        out_specs=out_specs,
        check_vma=False,
    )
```
